512 devices in a mesh: ctx: 64 (over y_lo, z, core), mp: 8 (over y_hi, x).
Axes of the slice: x: 4, y: 4 (y_hi: 2, y_lo: 2; y = y_hi * 2 + y_lo), z: 16, core: 2. Of those that a mesh axis runs over, the one named last changes fastest.
Arguments:
- sublayer_input: bfloat16 [8192, 4096], P('ctx'), may hold values from -16 to 16
- rotated_queries: bfloat16 [8192, 8192], P('ctx', 'mp'), may hold values from -5 to 5
- rotated_keys: bfloat16 [8192, 1024], P('ctx', 'mp'), may hold values from -5 to 5
- output_grad: bfloat16 [8192, 8192], P('ctx', 'mp'), may hold values from -6 to 6
- value_weight: bfloat16 [4096, 1024], P(None, 'mp'), may hold values from -0.09375 to 0.09375
- segment_ids: int32 [8192], replicated, may hold values from 0 to 3, never falling along the last dimension, each value on 1 to 6144 neighbouring positions
- label_positions: int32 [128], replicated, may hold values from 0 to 8191
Outputs:
- query_grad: bfloat16 [8192, 8192], P('ctx', 'mp')
- key_grad: bfloat16 [8192, 1024], P('ctx', 'mp')
- input_grad: bfloat16 [8192, 4096], P('ctx', 'mp')
- value_weight_grad: bfloat16 [4096, 1024], P('ctx', 'mp')
The draws below stay inside these ranges and needn't reach their ends.
Inputs may be any that keep to these rules, and one draw needn't show every extreme that they name: `segment_ids`: ids never fall along the slab; one trace takes exactly 6144 positions. `label_positions`: a position may appear more than once.
All inputs are finite; a program needn't handle non-finite values.
Results may differ from the reference program's by a relative error of at most 0.017.
Values may be sent and summed in bfloat16 or wider, within the bound.
No kernel may reach another device: no remote copies, remote signals or barrier semaphores. Data moves between devices by JAX's collectives and lax.ppermute only.
A program may use at most 64 MiB of HBM per device.

```python
import math
import jax
import jax.numpy as jnp
import numpy as np
from jax import lax

HEADS = 64
KV_HEADS = 8
HD = 128
D = 4096
DOCS = 4
LABELS = 128
TOKENS = 8192
LONGEST = 6144


def draw_rotated_queries(key, part):
    base = jax.random.truncated_normal(jax.random.fold_in(key, 21), -4.0, 4.0, (TOKENS, HEADS * HD), jnp.float32)
    return base.astype(jnp.bfloat16)


def draw_rotated_keys(key, part):
    base = jax.random.truncated_normal(jax.random.fold_in(key, 22), -4.0, 4.0, (TOKENS, KV_HEADS * HD), jnp.float32)
    return base.astype(jnp.bfloat16)


def place_ends(drawn, stream_key, least, top_value):
    index_at = [jax.random.randint(jax.random.fold_in(stream_key, axis), (), 0, length) for axis, length in enumerate(drawn.shape)]
    widest = drawn.shape.index(max(drawn.shape))
    next_to = index_at[:widest] + [(index_at[widest] + 1) % drawn.shape[widest]] + index_at[widest + 1:]
    return drawn.at[tuple(index_at)].set(least).at[tuple(next_to)].set(top_value)


def spiked(values, own_key, source, target, blocks, factor):
    def block_of(position):
        return (jnp.arange(values.shape[position]) // (values.shape[position] // blocks)).reshape((-1,) + (1,) * (values.ndim - 1 - position))

    one_side = jax.random.permutation(own_key, blocks)[block_of(target)]
    far = (block_of(target) + blocks // 2) % blocks
    return jnp.where((block_of(source) == one_side) | (block_of(source) == far), factor * values, values)


def block_scale(own_key, extent, cuts, smallest, high):
    gain, own = 1.0, jax.random.fold_in(own_key, 6)
    for axis_at, shards_of in cuts:
        heights = jnp.exp(jax.random.uniform(jax.random.fold_in(own, axis_at), (shards_of,), jnp.float32, smallest / len(cuts), high / len(cuts)))
        gain = gain * jnp.repeat(heights, extent[axis_at] // shards_of).reshape([-1 if axis == axis_at else 1 for axis in range(len(extent))])
    return gain


def profile(number_of, total, limit, skew):
    loads = [(1 << 20) // math.isqrt(grade ** skew) + 1 for grade in range(2, number_of + 1)]
    rest, holding = total - limit - (number_of - 1), [1] * (number_of - 1)
    while rest > 0:
        candidates = [i for i in range(number_of - 1) if holding[i] < limit]
        mass, remaining = sum([loads[i] for i in candidates]), rest
        for i in candidates:
            addition = min(limit - holding[i], max(1, remaining * loads[i] // mass), rest)
            holding[i] = holding[i] + addition
            rest = rest - addition
    return np.array([limit] + holding)


def uneven_parts(own_key, amount, total, reach, skew):
    if amount == 2:
        one = jax.random.randint(own_key, (), max(1, total - reach), min(reach, total - 1) + 1)
        return jnp.stack([one, total - one])
    sizes = jnp.asarray(profile(amount, total, reach, skew), jnp.int32)
    couples = (amount - 1) // 2
    source_of, receiver = sizes[1:1 + 2 * couples:2], sizes[2:2 + 2 * couples:2]
    slack = jnp.minimum(source_of - 1, reach - receiver)
    shifted = jax.random.randint(jax.random.fold_in(own_key, 1), (couples,), 0, 1 << 20) % (slack + 1)
    sizes = sizes.at[1:1 + 2 * couples:2].set(source_of - shifted).at[2:2 + 2 * couples:2].set(receiver + shifted)
    return sizes[jax.random.permutation(jax.random.fold_in(own_key, 2), amount)]


def centred(rng, dims, spread, reach, shards=(), kind=jnp.bfloat16):
    drawn = spread * jax.random.normal(rng, dims, jnp.float32)
    if shards:
        drawn = drawn * block_scale(rng, dims, shards, -0.22, 0.18)
    return jnp.clip(drawn, -reach, reach).astype(kind)


def bell_draw_with(key, shape, width, bound, split, heavy, held_as=jnp.bfloat16):
    drawn = width * jax.random.normal(key, shape, jnp.float32)
    if split:
        drawn = drawn * block_scale(key, shape, split, -0.22, 0.18)
    return jnp.clip(spiked(drawn, jax.random.fold_in(key, 3), *heavy), -bound, bound).astype(held_as)


def setup_inputs(seed: int = 0) -> dict:
    key_of = jax.random.split(jax.random.key(seed), 8)
    return {
        "sublayer_input": bell_draw_with(key_of[0], (TOKENS, D), 1.0, 16.0, ((0, 64),), (0, 1, 64, 4.0)),
        "rotated_queries": draw_rotated_queries(jax.random.fold_in(key_of[7], 71), 0),
        "rotated_keys": draw_rotated_keys(jax.random.fold_in(key_of[7], 71), 0),
        "output_grad": centred(key_of[3], (TOKENS, HEADS * HD), 1.0, 6.0, ((0, 64), (1, 8))),
        "value_weight": centred(key_of[4], (D, KV_HEADS * HD), D ** -0.5, 0.09375, ((1, 8),)),
        "segment_ids": jnp.searchsorted(jnp.cumsum(uneven_parts(key_of[5], DOCS, TOKENS, LONGEST, 2)), jnp.arange(TOKENS), side="right").astype(jnp.int32),
        "label_positions": place_ends(jax.random.randint(key_of[6], (LABELS,), 0, TOKENS), jax.random.fold_in(key_of[6], 1), 0, TOKENS - 1).astype(jnp.int32),
    }


NEGATIVE = -1.0e30


def reference(sublayer_input, rotated_queries, rotated_keys, output_grad, value_weight, segment_ids, label_positions):
    total_rows = sublayer_input.shape[0]
    group_size = HEADS // KV_HEADS
    score_scale = HD ** -0.5
    positions = jnp.arange(total_rows, dtype=jnp.int32)
    labelled = jnp.any(positions[:, None] == label_positions[None, :], axis=1)
    loss_weight = jnp.where(labelled, 4.0, 1.0).astype(jnp.float32)
    weighted = (output_grad.astype(jnp.float32) * loss_weight[:, None]).astype(jnp.bfloat16)
    values = jnp.dot(sublayer_input, value_weight, preferred_element_type=jnp.float32).astype(jnp.bfloat16)
    query_heads = rotated_queries.reshape(total_rows, KV_HEADS, group_size, HD).transpose(1, 2, 0, 3)
    grad_heads = weighted.reshape(total_rows, KV_HEADS, group_size, HD).transpose(1, 2, 0, 3)
    key_heads = rotated_keys.reshape(total_rows, KV_HEADS, HD).transpose(1, 0, 2)
    value_heads = values.reshape(total_rows, KV_HEADS, HD).transpose(1, 0, 2)
    query_block = 512 if total_rows % 512 == 0 else total_rows
    block_count = total_rows // query_block

    def per_head(operands):
        query_one, grad_one, key_one, value_one = operands
        key_full = key_one.astype(jnp.float32)
        value_full = value_one.astype(jnp.float32)

        def per_block(carry, block_index):
            key_sum, value_sum = carry
            block_start = (block_index * query_block).astype(jnp.int32)
            query_part = lax.dynamic_slice_in_dim(query_one, block_start, query_block, 1).astype(jnp.float32)
            grad_part = lax.dynamic_slice_in_dim(grad_one, block_start, query_block, 1).astype(jnp.float32)
            row_positions = block_start + jnp.arange(query_block, dtype=jnp.int32)
            row_segments = lax.dynamic_slice_in_dim(segment_ids, block_start, query_block)
            allowed = (row_segments[:, None] == segment_ids[None, :]) & (row_positions[:, None] >= positions[None, :])
            allowed = allowed[None, :, :]
            scores = jnp.einsum("gqd,kd->gqk", query_part, key_full) * score_scale
            masked = jnp.where(allowed, scores, NEGATIVE)
            row_top = jnp.max(masked, axis=-1, keepdims=True)
            exp_total = jnp.sum(jnp.where(allowed, jnp.exp(masked - row_top), 0.0), axis=-1, keepdims=True)
            log_total = row_top + jnp.log(exp_total)
            probabilities = jnp.where(allowed, jnp.exp(masked - log_total), 0.0)
            grad_probs = jnp.einsum("gqd,kd->gqk", grad_part, value_full)
            delta = jnp.sum(probabilities * grad_probs, axis=-1, keepdims=True)
            probs_low = lax.optimization_barrier(probabilities.astype(jnp.bfloat16))
            grad_scores = lax.optimization_barrier((probabilities * (grad_probs - delta) * score_scale).astype(jnp.bfloat16))
            probs_wide = probs_low.astype(jnp.float32)
            scores_wide = grad_scores.astype(jnp.float32)
            query_part_grad = jnp.einsum("gqk,kd->gqd", scores_wide, key_full).astype(jnp.bfloat16)
            key_sum = key_sum + jnp.einsum("gqk,gqd->kd", scores_wide, query_part)
            value_sum = value_sum + jnp.einsum("gqk,gqd->kd", probs_wide, grad_part)
            return (key_sum, value_sum), query_part_grad

        start_sums = (jnp.zeros((total_rows, HD), jnp.float32), jnp.zeros((total_rows, HD), jnp.float32))
        (key_sum, value_sum), query_blocks = lax.scan(per_block, start_sums, jnp.arange(block_count, dtype=jnp.int32))
        return key_sum, value_sum, query_blocks

    key_sums, value_sums, query_blocks = lax.map(per_head, (query_heads, grad_heads, key_heads, value_heads))
    query_grad = query_blocks.transpose(1, 3, 0, 2, 4).reshape(total_rows, HEADS * HD)
    key_grad = key_sums.transpose(1, 0, 2).reshape(total_rows, KV_HEADS * HD).astype(jnp.bfloat16)
    value_grad = value_sums.transpose(1, 0, 2).reshape(total_rows, KV_HEADS * HD).astype(jnp.bfloat16)
    input_grad = jnp.dot(value_grad, value_weight.T, preferred_element_type=jnp.float32).astype(jnp.bfloat16)
    value_weight_grad = jnp.dot(sublayer_input.T, value_grad, preferred_element_type=jnp.float32).astype(jnp.bfloat16)
    return query_grad, key_grad, input_grad, value_weight_grad
```

```python
import math

import jax
import jax.numpy as jnp
from jax import lax
from jax.experimental import pallas as pl
from jax.experimental.pallas import tpu as pltpu
from jax.sharding import PartitionSpec as P

HEADS = 64
KV_HEADS = 8
GROUP = HEADS // KV_HEADS
HD = 128
ROWS = 128
SCALE = HD ** (-0.5)
POWER = SCALE * math.log2(math.e)
FLOOR = -1e30
HIDDEN = -1e32
Y, Z, C = 2, 16, 2
TILE = 256
TILES = Z * ROWS // TILE
NT = (((1,), (1,)), ((), ()))
NN = (((1,), (0,)), ((), ()))


def at(y, z, c):
    return (y * Z + z) * C + c


Y_SWAP = [(i, i ^ (Z * C)) for i in range(Y * Z * C)]
C_SWAP = [(i, i ^ 1) for i in range(Y * Z * C)]
QUADS = [[at(y, z, c) for y in range(Y) for c in range(C)] for z in range(Z)]
LINES = [[at(y, z, c) for z in range(Z)] for y in range(Y) for c in range(C)]
CLASSES = [
    sorted(at((z + s) % 2, z, c) for z in range(Z)) for s in range(2) for c in range(C)
]


def dot(a, b, dims):
    return lax.dot_general(a, b, dims, preferred_element_type=jnp.float32)


def tile_first(place, tile):
    half = TILES // 2
    low = place[4] + 8 * tile
    high = place[5] + 8 * (tile - half)
    return jnp.where(tile < half, low, high) * ROWS


def doc_start(place, position):
    begin = jnp.zeros_like(position)
    for k in range(6, 9):
        begin = jnp.where(place[k] <= position, jnp.maximum(begin, place[k]), begin)
    return begin


def tile_state(place, j, tile):
    query_first = place[j] * ROWS
    key_first = tile_first(place, tile)
    key_last = key_first + 5 * ROWS - 1
    active = (key_first < query_first + ROWS) & (
        key_last >= doc_start(place, query_first)
    )
    return query_first, key_first, active


def tile_mask(place, query_first, key_first):
    row = lax.broadcasted_iota(jnp.int32, (TILE, ROWS), 0)
    key_position = key_first + row + jnp.where(row >= ROWS, 3 * ROWS, 0)
    query_position = query_first + lax.broadcasted_iota(jnp.int32, (TILE, ROWS), 1)
    begin = doc_start(place, query_position)
    return (key_position <= query_position) & (key_position >= begin)


def stats_kernel(place, qd, kv, out, top, total, inner):
    def query_block(j, _):
        top[...] = jnp.full(top.shape, FLOOR, jnp.float32)
        total[...] = jnp.zeros(total.shape, jnp.float32)
        inner[...] = jnp.zeros(inner.shape, jnp.float32)

        def key_tile(tile, _):
            query_first, key_first, active = tile_state(place, j, tile)

            @pl.when(active)
            def _():
                mask = tile_mask(place, query_first, key_first)
                rows = pl.ds(pl.multiple_of(tile * TILE, TILE), TILE)
                keys = kv[rows, :HD]
                values = kv[rows, HD:]
                for pair in range(GROUP // 2):
                    span = pl.ds(pair * 2 * ROWS, 2 * ROWS)
                    grad_span = pl.ds((GROUP + pair * 2) * ROWS, 2 * ROWS)
                    scores = dot(keys, qd[j, span, :], NT)
                    grad_probs = dot(values, qd[j, grad_span, :], NT)
                    for i in range(2):
                        head = 2 * pair + i
                        lanes = slice(i * ROWS, (i + 1) * ROWS)
                        s = jnp.where(mask, scores[:, lanes], HIDDEN)
                        s = s.reshape(TILE // 8, 8, ROWS)
                        g = grad_probs[:, lanes].reshape(TILE // 8, 8, ROWS)
                        old = top[head]
                        new = jnp.maximum(old, jnp.max(s, axis=0))
                        factor = jnp.exp2((old - new) * POWER)
                        p = jnp.exp2((s - new[None]) * POWER)
                        total[head] = total[head] * factor + jnp.sum(p, axis=0)
                        inner[head] = inner[head] * factor + jnp.sum(p * g, axis=0)
                        top[head] = new

            return 0

        lax.fori_loop(0, TILES, key_tile, 0)
        tops = top[...]
        best = jnp.max(tops, axis=1)
        weight = jnp.exp2((tops - best[:, None, :]) * POWER)
        out[0, j] = best
        out[1, j] = jnp.sum(total[...] * weight, axis=1)
        out[2, j] = jnp.sum(inner[...] * weight, axis=1)
        return 0

    lax.fori_loop(0, Y * C, query_block, 0)


def grads_kernel(
    place, stats, qd, kv, kt, dq, dkv, log_total, delta, probs, grad_scores, dqt, dkv_sum
):
    mine_y, mine_c = place[9], place[10]
    for j in range(Y * C):
        parts = []
        for r in range(Y * C):
            slot = 2 * (mine_y ^ (r & 1)) + (mine_c ^ (r >> 1))
            parts.append([stats[slot, k, j ^ r] for k in range(3)])
        best = parts[0][0]
        for part in parts[1:]:
            best = jnp.maximum(best, part[0])
        total = jnp.zeros_like(best)
        inner = jnp.zeros_like(best)
        for part in parts:
            weight = jnp.exp2((part[0] - best) * POWER)
            total += part[1] * weight
            inner += part[2] * weight
        log_total[j] = best * POWER + jnp.log(total) * math.log2(math.e)
        delta[j] = inner / total
    dkv_sum[...] = jnp.zeros(dkv_sum.shape, jnp.float32)

    def query_block(j, _):
        dqt[...] = jnp.zeros(dqt.shape, jnp.float32)

        def key_tile(tile, _):
            query_first, key_first, active = tile_state(place, j, tile)

            @pl.when(active)
            def _():
                mask = tile_mask(place, query_first, key_first)
                rows = pl.ds(pl.multiple_of(tile * TILE, TILE), TILE)
                keys = kv[rows, :HD]
                values = kv[rows, HD:]
                for pair in range(GROUP // 2):
                    span = pl.ds(pair * 2 * ROWS, 2 * ROWS)
                    grad_span = pl.ds((GROUP + pair * 2) * ROWS, 2 * ROWS)
                    scores = dot(keys, qd[j, span, :], NT)
                    grads = dot(values, qd[j, grad_span, :], NT)
                    for i in range(2):
                        head = 2 * pair + i
                        lanes = slice(i * ROWS, (i + 1) * ROWS)
                        whole = slice(head * ROWS, (head + 1) * ROWS)
                        x = scores[:, lanes] * POWER - log_total[j, pl.ds(head, 1), :]
                        p = jnp.exp2(jnp.where(mask, x, FLOOR))
                        probs[:, whole] = p.astype(jnp.bfloat16)
                        d = p * (grads[:, lanes] - delta[j, pl.ds(head, 1), :])
                        grad_scores[:, whole] = d.astype(jnp.bfloat16)
                weights = grad_scores[...]
                dqt[...] += dot(kt[:, rows], weights, NN)
                dkv_sum[rows, :HD] += dot(weights, qd[j, pl.ds(0, GROUP * ROWS), :], NN)
                dkv_sum[rows, HD:] += dot(
                    probs[...], qd[j, pl.ds(GROUP * ROWS, GROUP * ROWS), :], NN
                )

            return 0

        lax.fori_loop(0, TILES, key_tile, 0)
        for head in range(GROUP):
            lanes = slice(head * ROWS, (head + 1) * ROWS)
            dq[j, :, lanes] = (dqt[:, lanes].T * SCALE).astype(jnp.bfloat16)
        return 0

    lax.fori_loop(0, Y * C, query_block, 0)
    dkv[:, :HD] = (dkv_sum[:, :HD] * SCALE).astype(jnp.bfloat16)
    dkv[:, HD:] = dkv_sum[:, HD:].astype(jnp.bfloat16)


def on_device(
    sublayer_input,
    rotated_queries,
    rotated_keys,
    output_grad,
    value_weight,
    segment_ids,
    label_positions,
):
    bf16, f32 = jnp.bfloat16, jnp.float32
    context = lax.axis_index("ctx")
    mine_y, mine_z, mine_c = context // (Z * C), context // C % Z, context % C
    side = (mine_y + mine_z) % 2
    own_positions = context * ROWS + jnp.arange(ROWS, dtype=jnp.int32)
    labelled = jnp.any(own_positions[:, None] == label_positions[None, :], axis=1)
    loss_weight = jnp.where(labelled, 4.0, 1.0).astype(f32)
    weighted = (output_grad.astype(f32) * loss_weight[:, None]).astype(bf16)
    starts = [jnp.sum((segment_ids < k).astype(jnp.int32)) for k in range(1, 4)]
    place = jnp.stack(
        [
            at(mine_y ^ (j & 1), mine_z, mine_c ^ (j >> 1)).astype(jnp.int32)
            for j in range(Y * C)
        ]
        + [2 * side + mine_c, 2 * Z + 2 * (1 - side) + mine_c]
        + starts
        + [mine_y, mine_c]
    ).astype(jnp.int32)

    def by_head(x):
        return x.reshape(ROWS, GROUP, HD).transpose(1, 0, 2).reshape(GROUP * ROWS, HD)

    own = jnp.concatenate([by_head(rotated_queries), by_head(weighted)], axis=0)
    across = lax.ppermute(own, "ctx", Y_SWAP)
    values = jnp.dot(sublayer_input, value_weight, preferred_element_type=f32).astype(bf16)
    own_kv = jnp.concatenate([rotated_keys, values], axis=1)
    kv = lax.all_to_all(
        jnp.broadcast_to(own_kv[None], (Z,) + own_kv.shape),
        "ctx",
        0,
        0,
        axis_index_groups=CLASSES,
    ).reshape(Z * ROWS, 2 * HD)
    beside = lax.ppermute(jnp.stack([own, across]), "ctx", C_SWAP)
    qd = jnp.concatenate([own[None], across[None], beside], axis=0)

    smem = pl.BlockSpec(memory_space=pltpu.SMEM)
    vmem = pl.BlockSpec(memory_space=pltpu.VMEM)
    params = pltpu.CompilerParams(vmem_limit_bytes=48 * 1024 * 1024)
    stat = pltpu.VMEM((GROUP, 8, ROWS), f32)
    stats = pl.pallas_call(
        stats_kernel,
        out_shape=jax.ShapeDtypeStruct((3, Y * C, GROUP, ROWS), f32),
        in_specs=[smem, vmem, vmem],
        out_specs=vmem,
        scratch_shapes=[stat, stat, stat],
        compiler_params=params,
    )(place, qd, kv)
    all_stats = lax.all_gather(stats, "ctx", axis_index_groups=QUADS)
    kt = kv[:, :HD].T
    dq, dkv = pl.pallas_call(
        grads_kernel,
        out_shape=(
            jax.ShapeDtypeStruct((Y * C, ROWS, GROUP * HD), bf16),
            jax.ShapeDtypeStruct((Z * ROWS, 2 * HD), bf16),
        ),
        in_specs=[smem, vmem, vmem, vmem, vmem],
        out_specs=(vmem, vmem),
        scratch_shapes=[
            pltpu.VMEM((Y * C, GROUP, ROWS), f32),
            pltpu.VMEM((Y * C, GROUP, ROWS), f32),
            pltpu.VMEM((TILE, GROUP * ROWS), bf16),
            pltpu.VMEM((TILE, GROUP * ROWS), bf16),
            pltpu.VMEM((HD, GROUP * ROWS), f32),
            pltpu.VMEM((Z * ROWS, 2 * HD), f32),
        ],
        compiler_params=params,
    )(place, all_stats, qd, kv, kt)

    from_core = lax.ppermute(dq[2:], "ctx", C_SWAP).astype(f32)
    for_across = (dq[1].astype(f32) + from_core[1]).astype(bf16)
    from_across = lax.ppermute(for_across, "ctx", Y_SWAP).astype(f32)
    query_grad = (dq[0].astype(f32) + from_core[0] + from_across).astype(bf16)

    parts = lax.all_to_all(
        dkv.reshape(Z, ROWS, 2 * HD), "ctx", 0, 0, axis_index_groups=CLASSES
    )
    summed = jnp.sum(parts.astype(f32), axis=0).astype(bf16)
    key_grad = summed[:, :HD]
    value_grad = summed[:, HD:]

    mp_count = lax.axis_size("mp")
    width = value_weight.shape[0] // mp_count
    input_terms = jnp.einsum(
        "td,med->mte",
        value_grad,
        value_weight.reshape(mp_count, width, HD),
        preferred_element_type=f32,
    ).astype(bf16)
    input_parts = lax.all_to_all(input_terms, "mp", 0, 0)
    input_grad = jnp.sum(input_parts.astype(f32), axis=0).astype(bf16)

    term = lax.dot_general(
        sublayer_input, value_grad, (((0,), (0,)), ((), ())), preferred_element_type=f32
    ).astype(bf16)
    piece = term.shape[0] // (Y * Z * C)
    term = term.reshape(Y * Z, C, piece, HD)
    near = lax.ppermute(jnp.where(mine_c == 0, term[:, 1], term[:, 0]), "ctx", C_SWAP)
    term = jnp.where(mine_c == 0, term[:, 0], term[:, 1]).astype(f32) + near.astype(f32)
    term = term.astype(bf16).reshape(Y, Z, piece, HD)
    far = lax.ppermute(jnp.where(mine_y == 0, term[1], term[0]), "ctx", Y_SWAP)
    term = jnp.where(mine_y == 0, term[0], term[1]).astype(f32) + far.astype(f32)
    pieces = lax.all_to_all(term.astype(bf16), "ctx", 0, 0, axis_index_groups=LINES)
    value_weight_grad = jnp.sum(pieces.astype(f32), axis=0).astype(bf16)
    return (query_grad, key_grad, input_grad, value_weight_grad)


def solution(mesh):
    placed = (
        P("ctx", None),
        P("ctx", "mp"),
        P("ctx", "mp"),
        P("ctx", "mp"),
        P(None, "mp"),
        P(),
        P(),
    )
    return jax.shard_map(
        on_device,
        mesh=mesh,
        in_specs=placed,
        out_specs=(P("ctx", "mp"), P("ctx", "mp"), P("ctx", "mp"), P("ctx", "mp")),
        check_vma=False,
    )
```

```python
import math

import jax
import jax.numpy as jnp
from jax import lax
from jax.experimental import pallas as pl
from jax.experimental.pallas import tpu as pltpu
from jax.sharding import PartitionSpec as P

HEADS = 64
KV_HEADS = 8
GROUP = HEADS // KV_HEADS
HD = 128
ROWS = 128
SCALE = HD ** (-0.5)
POWER = SCALE * math.log2(math.e)
FLOOR = -1e30
HIDDEN = -1e32
Y, Z, C = 2, 16, 2
TILE = 256
TILES = Z * ROWS // TILE
NT = (((1,), (1,)), ((), ()))
NN = (((1,), (0,)), ((), ()))
TN = (((0,), (0,)), ((), ()))


def at(y, z, c):
    return (y * Z + z) * C + c


Y_SWAP = [(i, i ^ (Z * C)) for i in range(Y * Z * C)]
C_SWAP = [(i, i ^ 1) for i in range(Y * Z * C)]
QUADS = [[at(y, z, c) for y in range(Y) for c in range(C)] for z in range(Z)]
LINES = [[at(y, z, c) for z in range(Z)] for y in range(Y) for c in range(C)]
COLUMNS = [
    [at(y, z + 4 * k, c) for k in range(Z // 4)]
    for y in range(Y)
    for z in range(4)
    for c in range(C)
]
BASES = [0, 8, 12, 4]
GROUPS = (4, 4, 4, 2, 2)
PARTS = Y * C + len(GROUPS)


def along_z(value, distance):
    pairs = [
        (at(y, z, c), at((y + distance) % 2, (z + distance) % Z, c))
        for y in range(Y)
        for z in range(Z)
        for c in range(C)
    ]
    return lax.ppermute(value, "ctx", pairs)


def dot(a, b, dims):
    return lax.dot_general(a, b, dims, preferred_element_type=jnp.float32)


def tile_first(place, tile):
    half = TILES // 2
    low = place[4] + 8 * tile
    high = place[5] + 8 * (tile - half)
    return jnp.where(tile < half, low, high) * ROWS


def tile_slots(place, tile):
    half = TILES // 2
    residue = jnp.where(tile < half, place[11], 1 - place[11]) - place[12] + Z
    within = lax.rem(tile, half)
    return place[13 + lax.rem(residue, 4)] + within, place[13 + lax.rem(residue + 2, 4)] + within


def slot_rows(slot):
    return pl.ds(pl.multiple_of(slot * ROWS, ROWS), ROWS)


def gather_parts(refs, qd, kv):
    for j in range(Y * C):
        qd[j] = refs[j][...]
    first = 0
    for part in refs[Y * C :]:
        count = part.shape[0]
        for i in range(count):
            kv[(first + i) * ROWS : (first + i + 1) * ROWS, :] = part[i]
        first += count


def doc_start(place, position):
    begin = jnp.zeros_like(position)
    for k in range(6, 9):
        begin = jnp.where(place[k] <= position, jnp.maximum(begin, place[k]), begin)
    return begin


def tile_state(place, j, tile):
    query_first = place[j] * ROWS
    key_first = tile_first(place, tile)
    key_last = key_first + 5 * ROWS - 1
    active = (key_first < query_first + ROWS) & (
        key_last >= doc_start(place, query_first)
    )
    return query_first, key_first, active


def tile_mask(place, query_first, key_first):
    row = lax.broadcasted_iota(jnp.int32, (TILE, ROWS), 0)
    key_position = key_first + row + jnp.where(row >= ROWS, 3 * ROWS, 0)
    query_position = query_first + lax.broadcasted_iota(jnp.int32, (TILE, ROWS), 1)
    begin = doc_start(place, query_position)
    return (key_position <= query_position) & (key_position >= begin)


def stats_kernel(place, *refs):
    out, qd, kv, top, total, inner = refs[PARTS:]
    gather_parts(refs[:PARTS], qd, kv)

    def query_block(j, _):
        top[...] = jnp.full(top.shape, FLOOR, jnp.float32)
        total[...] = jnp.zeros(total.shape, jnp.float32)
        inner[...] = jnp.zeros(inner.shape, jnp.float32)

        def key_tile(tile, _):
            query_first, key_first, active = tile_state(place, j, tile)

            @pl.when(active)
            def _():
                mask = tile_mask(place, query_first, key_first)
                one, two = (slot_rows(slot) for slot in tile_slots(place, tile))
                keys = jnp.concatenate([kv[one, :HD], kv[two, :HD]], axis=0)
                values = jnp.concatenate([kv[one, HD:], kv[two, HD:]], axis=0)
                for pair in range(GROUP // 2):
                    span = pl.ds(pair * 2 * ROWS, 2 * ROWS)
                    grad_span = pl.ds((GROUP + pair * 2) * ROWS, 2 * ROWS)
                    scores = dot(keys, qd[j, span, :], NT)
                    grad_probs = dot(values, qd[j, grad_span, :], NT)
                    for i in range(2):
                        head = 2 * pair + i
                        lanes = slice(i * ROWS, (i + 1) * ROWS)
                        s = jnp.where(mask, scores[:, lanes], HIDDEN)
                        s = s.reshape(TILE // 8, 8, ROWS)
                        g = grad_probs[:, lanes].reshape(TILE // 8, 8, ROWS)
                        old = top[head]
                        new = jnp.maximum(old, jnp.max(s, axis=0))
                        factor = jnp.exp2((old - new) * POWER)
                        p = jnp.exp2((s - new[None]) * POWER)
                        total[head] = total[head] * factor + jnp.sum(p, axis=0)
                        inner[head] = inner[head] * factor + jnp.sum(p * g, axis=0)
                        top[head] = new

            return 0

        lax.fori_loop(0, TILES, key_tile, 0)
        tops = top[...]
        best = jnp.max(tops, axis=1)
        weight = jnp.exp2((tops - best[:, None, :]) * POWER)
        out[0, j] = best
        out[1, j] = jnp.sum(total[...] * weight, axis=1)
        out[2, j] = jnp.sum(inner[...] * weight, axis=1)
        return 0

    lax.fori_loop(0, Y * C, query_block, 0)


def grads_kernel(place, stats, *refs):
    dq, dq_core = refs[PARTS : PARTS + 2]
    sums, scratch = refs[PARTS + 2 : PARTS + 2 + len(GROUPS)], refs[PARTS + 2 + len(GROUPS) :]
    qd, kv, kt, log_total, delta, probs, grad_scores, dqt, dkv_sum = scratch
    gather_parts(refs[:PARTS], qd, kv)
    for slot in range(Z):
        rows = slice(slot * ROWS, (slot + 1) * ROWS)
        kt[slot] = kv[rows, :HD].T
    mine_y, mine_c = place[9], place[10]
    for j in range(Y * C):
        parts = []
        for r in range(Y * C):
            slot = 2 * (mine_y ^ (r & 1)) + (mine_c ^ (r >> 1))
            parts.append([stats[slot, k, j ^ r] for k in range(3)])
        best = parts[0][0]
        for part in parts[1:]:
            best = jnp.maximum(best, part[0])
        total = jnp.zeros_like(best)
        inner = jnp.zeros_like(best)
        for part in parts:
            weight = jnp.exp2((part[0] - best) * POWER)
            total += part[1] * weight
            inner += part[2] * weight
        log_total[j] = best * POWER + jnp.log(total) * math.log2(math.e)
        delta[j] = inner / total
    dkv_sum[...] = jnp.zeros(dkv_sum.shape, jnp.float32)

    def query_block(j, _):
        dqt[...] = jnp.zeros(dqt.shape, jnp.float32)

        def key_tile(tile, _):
            query_first, key_first, active = tile_state(place, j, tile)

            @pl.when(active)
            def _():
                mask = tile_mask(place, query_first, key_first)
                one, two = (slot_rows(slot) for slot in tile_slots(place, tile))
                keys = jnp.concatenate([kv[one, :HD], kv[two, :HD]], axis=0)
                values = jnp.concatenate([kv[one, HD:], kv[two, HD:]], axis=0)
                for pair in range(GROUP // 2):
                    span = pl.ds(pair * 2 * ROWS, 2 * ROWS)
                    grad_span = pl.ds((GROUP + pair * 2) * ROWS, 2 * ROWS)
                    scores = dot(keys, qd[j, span, :], NT)
                    grads = dot(values, qd[j, grad_span, :], NT)
                    for i in range(2):
                        head = 2 * pair + i
                        lanes = slice(i * ROWS, (i + 1) * ROWS)
                        whole = slice(head * ROWS, (head + 1) * ROWS)
                        x = scores[:, lanes] * POWER - log_total[j, pl.ds(head, 1), :]
                        p = jnp.exp2(jnp.where(mask, x, FLOOR))
                        probs[:, whole] = p.astype(jnp.bfloat16)
                        d = p * (grads[:, lanes] - delta[j, pl.ds(head, 1), :])
                        grad_scores[:, whole] = d.astype(jnp.bfloat16)
                weights = grad_scores[...]
                slots = tile_slots(place, tile)
                keys_t = jnp.concatenate([kt[slots[0]], kt[slots[1]]], axis=1)
                dqt[...] += dot(keys_t, weights, NN)
                key_term = dot(weights, qd[j, pl.ds(0, GROUP * ROWS), :], NN)
                value_term = dot(probs[...], qd[j, pl.ds(GROUP * ROWS, GROUP * ROWS), :], NN)
                for i, rows in enumerate((one, two)):
                    dkv_sum[rows, :HD] += key_term[i * ROWS : (i + 1) * ROWS]
                    dkv_sum[rows, HD:] += value_term[i * ROWS : (i + 1) * ROWS]

            return 0

        lax.fori_loop(0, TILES, key_tile, 0)
        for half, place_of in enumerate((dq, dq_core)):

            @pl.when(j // 2 == half)
            def _():
                for head in range(GROUP):
                    lanes = slice(head * ROWS, (head + 1) * ROWS)
                    turned = dqt[:, lanes].T * SCALE
                    place_of[lax.rem(j, 2), :, lanes] = turned.astype(jnp.bfloat16)

        return 0

    lax.fori_loop(0, Y * C, query_block, 0)
    slot = 0
    for part in sums:
        for i in range(part.shape[0]):
            rows = slice(slot * ROWS, (slot + 1) * ROWS)
            part[i, :, :HD] = (dkv_sum[rows, :HD] * SCALE).astype(jnp.bfloat16)
            part[i, :, HD:] = dkv_sum[rows, HD:].astype(jnp.bfloat16)
            slot += 1


def own_kv_kernel(inputs, weight, keys, out):
    values = dot(inputs[...], weight[...], NN).astype(jnp.bfloat16)
    for k in range(out.shape[0]):
        out[k, :, :HD] = keys[...]
        out[k, :, HD:] = values


def own_queries_kernel(index, labels, segments, queries, grads, out, place):
    context = index[0]
    y, z, c = context // (Z * C), lax.rem(context // C, Z), lax.rem(context, C)
    side = lax.rem(y + z, 2)
    for j in range(Y * C):
        place[j] = at(y ^ (j & 1), z, c ^ (j >> 1))
    place[4] = 2 * side + c
    place[5] = 2 * Z + 2 * (1 - side) + c
    for k in range(1, 4):
        before = jnp.where(segments[...] < k, 1.0, 0.0).astype(jnp.float32)
        place[5 + k] = jnp.sum(before).astype(jnp.int32)
    for i, value in enumerate((y, c, side, z)):
        place[9 + i] = value
    for i, base in enumerate(BASES):
        place[13 + i] = base
    position = context * ROWS + lax.broadcasted_iota(
        jnp.int32, (ROWS, labels.shape[1]), 0
    )
    labelled = jnp.where(position == labels[...], 3.0, 0.0).astype(jnp.float32)
    weight = 1.0 + jnp.max(labelled, axis=1, keepdims=True)
    for head in range(GROUP):
        lanes = slice(head * HD, (head + 1) * HD)
        out[head * ROWS : (head + 1) * ROWS] = queries[:, lanes]
        weighted = grads[:, lanes].astype(jnp.float32) * weight
        out[(GROUP + head) * ROWS : (GROUP + head + 1) * ROWS] = weighted.astype(jnp.bfloat16)


def weight_kernel(place, inputs, grads, kept, sent):
    total = dot(grads[...], inputs[...], TN)
    width = kept.shape[1]
    first = place[10] == 0
    for i in range(kept.shape[0]):
        turned = total[:, i * C * width : (i + 1) * C * width].T
        low, high = turned[:width], turned[width:]
        kept[i] = jnp.where(first, low, high).astype(jnp.bfloat16)
        sent[i] = jnp.where(first, high, low).astype(jnp.bfloat16)


def on_device(
    sublayer_input,
    rotated_queries,
    rotated_keys,
    output_grad,
    value_weight,
    segment_ids,
    label_positions,
):
    bf16, f32 = jnp.bfloat16, jnp.float32
    context = lax.axis_index("ctx")
    mine_y, mine_c = context // (Z * C), context % C
    smem = pl.BlockSpec(memory_space=pltpu.SMEM)
    vmem = pl.BlockSpec(memory_space=pltpu.VMEM)
    params = pltpu.CompilerParams(vmem_limit_bytes=24 * 1024 * 1024)
    column = pl.pallas_call(
        own_kv_kernel,
        out_shape=jax.ShapeDtypeStruct((Z // 4, ROWS, 2 * HD), bf16),
        in_specs=[vmem] * 3,
        out_specs=vmem,
        compiler_params=params,
    )(sublayer_input, value_weight, rotated_keys)
    column, output_grad, rotated_queries = lax.optimization_barrier(
        (column, output_grad, rotated_queries)
    )
    column = lax.all_to_all(column, "ctx", 0, 0, axis_index_groups=COLUMNS)

    own, place = pl.pallas_call(
        own_queries_kernel,
        out_shape=(
            jax.ShapeDtypeStruct((2 * GROUP * ROWS, HD), bf16),
            jax.ShapeDtypeStruct((13 + len(BASES),), jnp.int32),
        ),
        in_specs=[smem] + [vmem] * 4,
        out_specs=(vmem, smem),
        compiler_params=params,
    )(
        context.astype(jnp.int32).reshape(1),
        label_positions[None],
        segment_ids.reshape(-1, HD),
        rotated_queries,
        output_grad,
    )
    across = lax.ppermute(own, "ctx", Y_SWAP)
    beside = lax.ppermute(own, "ctx", C_SWAP)
    plane = Y * C
    column, beside = lax.optimization_barrier((column, beside))
    kv = [
        column,
        along_z(column, 1),
        along_z(column, -1),
        along_z(column[:2], 2),
        along_z(column[2:], -2),
    ]
    corner = lax.ppermute(across, "ctx", C_SWAP)
    operands = [own, across, beside, corner]
    operands += kv
    stat = pltpu.VMEM((GROUP, 8, ROWS), f32)
    all_qd = pltpu.VMEM((plane, 2 * GROUP * ROWS, HD), bf16)
    all_kv = pltpu.VMEM((Z * ROWS, 2 * HD), bf16)
    stats = pl.pallas_call(
        stats_kernel,
        out_shape=jax.ShapeDtypeStruct((3, plane, GROUP, ROWS), f32),
        in_specs=[smem] + [vmem] * PARTS,
        out_specs=vmem,
        scratch_shapes=[all_qd, all_kv, stat, stat, stat],
        compiler_params=params,
    )(place, *operands)
    all_stats = lax.all_gather(stats, "ctx", axis_index_groups=QUADS)
    dq, dq_core, *sums = pl.pallas_call(
        grads_kernel,
        out_shape=[jax.ShapeDtypeStruct((2, ROWS, GROUP * HD), bf16)] * 2
        + [jax.ShapeDtypeStruct((n, ROWS, 2 * HD), bf16) for n in GROUPS],
        in_specs=[smem, vmem] + [vmem] * PARTS,
        out_specs=[vmem] * (2 + len(GROUPS)),
        scratch_shapes=[
            all_qd,
            all_kv,
            pltpu.VMEM((Z, HD, ROWS), bf16),
            pltpu.VMEM((plane, GROUP, ROWS), f32),
            pltpu.VMEM((plane, GROUP, ROWS), f32),
            pltpu.VMEM((TILE, GROUP * ROWS), bf16),
            pltpu.VMEM((TILE, GROUP * ROWS), bf16),
            pltpu.VMEM((HD, GROUP * ROWS), f32),
            pltpu.VMEM((Z * ROWS, 2 * HD), f32),
        ],
        compiler_params=params,
    )(place, all_stats, *operands)

    back = [along_z(part, d) for part, d in zip(sums[1:], (-1, 1, -2, 2))]
    back[2], dq_core = lax.optimization_barrier((back[2], dq_core))
    from_core = lax.ppermute(dq_core, "ctx", C_SWAP)
    last = jnp.concatenate(back[2:], axis=0)
    column = sums[0].astype(f32) + back[0].astype(f32) + back[1].astype(f32) + last.astype(f32)
    column, from_core = lax.optimization_barrier((column.astype(bf16), from_core))
    from_core = from_core.astype(f32)
    for_across = (dq[1].astype(f32) + from_core[1]).astype(bf16)
    from_across = lax.ppermute(for_across, "ctx", Y_SWAP).astype(f32)
    query_grad = (dq[0].astype(f32) + from_core[0] + from_across).astype(bf16)
    column = lax.all_to_all(column, "ctx", 0, 0, axis_index_groups=COLUMNS)
    summed = jnp.sum(column.astype(f32), axis=0).astype(bf16)
    key_grad = summed[:, :HD]
    value_grad = summed[:, HD:]

    mp_count = lax.axis_size("mp")
    width = value_weight.shape[0] // mp_count
    input_terms = jnp.einsum(
        "td,med->mte",
        value_grad,
        value_weight.reshape(mp_count, width, HD),
        preferred_element_type=f32,
    ).astype(bf16)
    input_parts = lax.all_to_all(input_terms, "mp", 0, 0)
    input_grad = jnp.sum(input_parts.astype(f32), axis=0).astype(bf16)

    piece = sublayer_input.shape[1] // (Y * Z * C)
    kept, sent = pl.pallas_call(
        weight_kernel,
        out_shape=[jax.ShapeDtypeStruct((Y * Z, piece, HD), bf16)] * C,
        in_specs=[smem, vmem, vmem],
        out_specs=[vmem] * C,
        compiler_params=params,
    )(place, sublayer_input, value_grad)
    near = lax.ppermute(sent, "ctx", C_SWAP)
    term = (kept.astype(f32) + near.astype(f32)).astype(bf16).reshape(Y, Z, piece, HD)
    far = lax.ppermute(jnp.where(mine_y == 0, term[1], term[0]), "ctx", Y_SWAP)
    term = jnp.where(mine_y == 0, term[0], term[1]).astype(f32) + far.astype(f32)
    term = term.astype(bf16)
    pieces = lax.all_to_all(term, "ctx", 0, 0, axis_index_groups=LINES)
    value_weight_grad = jnp.sum(pieces.astype(f32), axis=0).astype(bf16)
    return (query_grad, key_grad, input_grad, value_weight_grad)


def solution(mesh):
    placed = (
        P("ctx", None),
        P("ctx", "mp"),
        P("ctx", "mp"),
        P("ctx", "mp"),
        P(None, "mp"),
        P(),
        P(),
    )
    return jax.shard_map(
        on_device,
        mesh=mesh,
        in_specs=placed,
        out_specs=(P("ctx", "mp"), P("ctx", "mp"), P("ctx", "mp"), P("ctx", "mp")),
        check_vma=False,
    )
```

```python
import math

import jax
import jax.numpy as jnp
from jax import lax
from jax.experimental import pallas as pl
from jax.experimental.pallas import tpu as pltpu
from jax.sharding import PartitionSpec as P

HEADS = 64
KV_HEADS = 8
GROUP = HEADS // KV_HEADS
HD = 128
ROWS = 128
SCALE = HD ** (-0.5)
POWER = SCALE * math.log2(math.e)
FLOOR = -1e30
HIDDEN = -1e32
Y, Z, C = 2, 16, 2
TILE = 512
BLOCKS = TILE // ROWS
TILES = Z * ROWS // TILE
NT = (((1,), (1,)), ((), ()))
NN = (((1,), (0,)), ((), ()))
TN = (((0,), (0,)), ((), ()))


def at(y, z, c):
    return (y * Z + z) * C + c


Y_SWAP = [(i, i ^ (Z * C)) for i in range(Y * Z * C)]
C_SWAP = [(i, i ^ 1) for i in range(Y * Z * C)]
QUADS = [[at(y, z, c) for y in range(Y) for c in range(C)] for z in range(Z)]
X = 4
X_GROUPS = [[h * X + x for x in range(X)] for h in range(2)]
H_SWAP = [(i, (i + X) % (2 * X)) for i in range(2 * X)]
LINES = [[at(y, z, c) for z in range(Z)] for y in range(Y) for c in range(C)]
COLUMNS = [
    [at(y, z + 4 * k, c) for k in range(Z // 4)]
    for y in range(Y)
    for z in range(4)
    for c in range(C)
]
BASES = [0, 8, 12, 4]
GROUPS = (4, 4, 4, 2, 2)
PARTS = Y * C + len(GROUPS)


def along_z(value, distance):
    pairs = [
        (at(y, z, c), at((y + distance) % 2, (z + distance) % Z, c))
        for y in range(Y)
        for z in range(Z)
        for c in range(C)
    ]
    return lax.ppermute(value, "ctx", pairs)


def dot(a, b, dims):
    return lax.dot_general(a, b, dims, preferred_element_type=jnp.float32)


def tile_first(place, tile):
    half = TILES // 2
    low = place[4] + 4 * BLOCKS * tile
    high = place[5] + 4 * BLOCKS * (tile - half)
    return jnp.where(tile < half, low, high) * ROWS


def tile_slots(place, tile):
    half = TILES // 2
    residue = jnp.where(tile < half, place[11], 1 - place[11]) - place[12] + Z
    within = lax.rem(tile, half) * (BLOCKS // 2)
    bases = [place[13 + lax.rem(residue + 2 * i, 4)] for i in range(2)]
    return [bases[i % 2] + within + i // 2 for i in range(BLOCKS)]


def slot_rows(slot):
    return pl.ds(pl.multiple_of(slot * ROWS, ROWS), ROWS)


def gather_parts(refs, qd, kv):
    for j in range(Y * C):
        qd[j] = refs[j][...]
    first = 0
    for part in refs[Y * C :]:
        count = part.shape[0]
        for i in range(count):
            kv[(first + i) * ROWS : (first + i + 1) * ROWS, :] = part[i]
        first += count


def doc_start(place, position):
    begin = jnp.zeros_like(position)
    for k in range(6, 9):
        begin = jnp.where(place[k] <= position, jnp.maximum(begin, place[k]), begin)
    return begin


def tile_state(place, j, tile):
    query_first = place[j] * ROWS
    key_first = tile_first(place, tile)
    key_last = key_first + (4 * BLOCKS - 3) * ROWS - 1
    active = (key_first < query_first + ROWS) & (
        key_last >= doc_start(place, query_first)
    )
    return query_first, key_first, active


def tile_mask(place, query_first, key_first):
    row = lax.broadcasted_iota(jnp.int32, (TILE, ROWS), 0)
    key_position = key_first + row + row // ROWS * (3 * ROWS)
    query_position = query_first + lax.broadcasted_iota(jnp.int32, (TILE, ROWS), 1)
    begin = doc_start(place, query_position)
    return (key_position <= query_position) & (key_position >= begin)


def stats_kernel(place, *refs):
    out, qd, kv, top, total, inner = refs[PARTS:]
    gather_parts(refs[:PARTS], qd, kv)

    def query_block(j, _):
        top[...] = jnp.full(top.shape, FLOOR, jnp.float32)
        total[...] = jnp.zeros(total.shape, jnp.float32)
        inner[...] = jnp.zeros(inner.shape, jnp.float32)

        def key_tile(tile, _):
            query_first, key_first, active = tile_state(place, j, tile)

            @pl.when(active)
            def _():
                mask = tile_mask(place, query_first, key_first)
                slots = tile_slots(place, tile)
                spans = [slot_rows(slot) for slot in slots]
                keys = jnp.concatenate([kv[rows, :HD] for rows in spans], axis=0)
                values = jnp.concatenate([kv[rows, HD:] for rows in spans], axis=0)
                for pair in range(GROUP // 2):
                    span = pl.ds(pair * 2 * ROWS, 2 * ROWS)
                    grad_span = pl.ds((GROUP + pair * 2) * ROWS, 2 * ROWS)
                    scores = dot(keys, qd[j, span, :], NT)
                    grad_probs = dot(values, qd[j, grad_span, :], NT)
                    for i in range(2):
                        head = 2 * pair + i
                        lanes = slice(i * ROWS, (i + 1) * ROWS)
                        s = jnp.where(mask, scores[:, lanes], HIDDEN)
                        s = s.reshape(TILE // 8, 8, ROWS)
                        g = grad_probs[:, lanes].reshape(TILE // 8, 8, ROWS)
                        old = top[head]
                        new = jnp.maximum(old, jnp.max(s, axis=0))
                        factor = jnp.exp2((old - new) * POWER)
                        p = jnp.exp2((s - new[None]) * POWER)
                        total[head] = total[head] * factor + jnp.sum(p, axis=0)
                        inner[head] = inner[head] * factor + jnp.sum(p * g, axis=0)
                        top[head] = new

            return 0

        lax.fori_loop(0, TILES, key_tile, 0)
        tops = top[...]
        best = jnp.max(tops, axis=1)
        weight = jnp.exp2((tops - best[:, None, :]) * POWER)
        out[0, j] = best
        out[1, j] = jnp.sum(total[...] * weight, axis=1)
        out[2, j] = jnp.sum(inner[...] * weight, axis=1)
        return 0

    lax.fori_loop(0, Y * C, query_block, 0)


def grads_kernel(place, stats, *refs):
    dq, dq_core = refs[PARTS : PARTS + 2]
    sums, scratch = refs[PARTS + 2 : PARTS + 2 + len(GROUPS)], refs[PARTS + 2 + len(GROUPS) :]
    qd, kv, kt, log_total, delta, probs, grad_scores, dqt, dkv_sum = scratch
    gather_parts(refs[:PARTS], qd, kv)
    for slot in range(Z):
        rows = slice(slot * ROWS, (slot + 1) * ROWS)
        kt[slot] = kv[rows, :HD].T
    mine_y, mine_c = place[9], place[10]
    for j in range(Y * C):
        parts = []
        for r in range(Y * C):
            slot = 2 * (mine_y ^ (r & 1)) + (mine_c ^ (r >> 1))
            parts.append([stats[slot, k, j ^ r] for k in range(3)])
        best = parts[0][0]
        for part in parts[1:]:
            best = jnp.maximum(best, part[0])
        total = jnp.zeros_like(best)
        inner = jnp.zeros_like(best)
        for part in parts:
            weight = jnp.exp2((part[0] - best) * POWER)
            total += part[1] * weight
            inner += part[2] * weight
        log_total[j] = best * POWER + jnp.log(total) * math.log2(math.e)
        delta[j] = inner / total
    dkv_sum[...] = jnp.zeros(dkv_sum.shape, jnp.float32)

    def query_block(j, _):
        dqt[...] = jnp.zeros(dqt.shape, jnp.float32)

        def key_tile(tile, _):
            query_first, key_first, active = tile_state(place, j, tile)

            @pl.when(active)
            def _():
                mask = tile_mask(place, query_first, key_first)
                slots = tile_slots(place, tile)
                spans = [slot_rows(slot) for slot in slots]
                keys = jnp.concatenate([kv[rows, :HD] for rows in spans], axis=0)
                values = jnp.concatenate([kv[rows, HD:] for rows in spans], axis=0)
                for pair in range(GROUP // 2):
                    span = pl.ds(pair * 2 * ROWS, 2 * ROWS)
                    grad_span = pl.ds((GROUP + pair * 2) * ROWS, 2 * ROWS)
                    scores = dot(keys, qd[j, span, :], NT)
                    grads = dot(values, qd[j, grad_span, :], NT)
                    for i in range(2):
                        head = 2 * pair + i
                        lanes = slice(i * ROWS, (i + 1) * ROWS)
                        whole = slice(head * ROWS, (head + 1) * ROWS)
                        x = scores[:, lanes] * POWER - log_total[j, pl.ds(head, 1), :]
                        p = jnp.exp2(jnp.where(mask, x, FLOOR))
                        probs[:, whole] = p.astype(jnp.bfloat16)
                        d = p * (grads[:, lanes] - delta[j, pl.ds(head, 1), :])
                        grad_scores[:, whole] = d.astype(jnp.bfloat16)
                weights = grad_scores[...]
                keys_t = jnp.concatenate([kt[slot] for slot in slots], axis=1)
                dqt[...] += dot(keys_t, weights, NN)
                key_term = dot(weights, qd[j, pl.ds(0, GROUP * ROWS), :], NN)
                value_term = dot(probs[...], qd[j, pl.ds(GROUP * ROWS, GROUP * ROWS), :], NN)
                for i, rows in enumerate(spans):
                    dkv_sum[rows, :HD] += key_term[i * ROWS : (i + 1) * ROWS]
                    dkv_sum[rows, HD:] += value_term[i * ROWS : (i + 1) * ROWS]

            return 0

        lax.fori_loop(0, TILES, key_tile, 0)
        for half, place_of in enumerate((dq, dq_core)):

            @pl.when(j // 2 == half)
            def _():
                for head in range(GROUP):
                    lanes = slice(head * ROWS, (head + 1) * ROWS)
                    turned = dqt[:, lanes].T * SCALE
                    place_of[lax.rem(j, 2), :, lanes] = turned.astype(jnp.bfloat16)

        return 0

    lax.fori_loop(0, Y * C, query_block, 0)
    slot = 0
    for part in sums:
        for i in range(part.shape[0]):
            rows = slice(slot * ROWS, (slot + 1) * ROWS)
            part[i, :, :HD] = (dkv_sum[rows, :HD] * SCALE).astype(jnp.bfloat16)
            part[i, :, HD:] = dkv_sum[rows, HD:].astype(jnp.bfloat16)
            slot += 1


def own_kv_kernel(inputs, weight, keys, out):
    values = dot(inputs[...], weight[...], NN).astype(jnp.bfloat16)
    for k in range(out.shape[0]):
        out[k, :, :HD] = keys[...]
        out[k, :, HD:] = values


def own_queries_kernel(index, labels, segments, queries, grads, out, place):
    context = index[0]
    y, z, c = context // (Z * C), lax.rem(context // C, Z), lax.rem(context, C)
    side = lax.rem(y + z, 2)
    for j in range(Y * C):
        place[j] = at(y ^ (j & 1), z, c ^ (j >> 1))
    place[4] = 2 * side + c
    place[5] = 2 * Z + 2 * (1 - side) + c
    for k in range(1, 4):
        before = jnp.where(segments[...] < k, 1.0, 0.0).astype(jnp.float32)
        place[5 + k] = jnp.sum(before).astype(jnp.int32)
    for i, value in enumerate((y, c, side, z)):
        place[9 + i] = value
    for i, base in enumerate(BASES):
        place[13 + i] = base
    position = context * ROWS + lax.broadcasted_iota(
        jnp.int32, (ROWS, labels.shape[1]), 0
    )
    labelled = jnp.where(position == labels[...], 3.0, 0.0).astype(jnp.float32)
    weight = 1.0 + jnp.max(labelled, axis=1, keepdims=True)
    for head in range(GROUP):
        lanes = slice(head * HD, (head + 1) * HD)
        out[head * ROWS : (head + 1) * ROWS] = queries[:, lanes]
        weighted = grads[:, lanes].astype(jnp.float32) * weight
        out[(GROUP + head) * ROWS : (GROUP + head + 1) * ROWS] = weighted.astype(jnp.bfloat16)


def finish_kernel(place, parts, inputs, weight, key_grad, kept, sent, terms):
    summed = parts[0].astype(jnp.float32)
    for i in range(1, parts.shape[0]):
        summed += parts[i].astype(jnp.float32)
    summed = summed.astype(jnp.bfloat16)
    key_grad[...] = summed[:, :HD]
    value_grad = summed[:, HD:]
    total = dot(value_grad, inputs[...], TN)
    width = kept.shape[1]
    first = place[10] == 0
    for i in range(kept.shape[0]):
        turned = total[:, i * C * width : (i + 1) * C * width].T
        low, high = turned[:width], turned[width:]
        kept[i] = jnp.where(first, low, high).astype(jnp.bfloat16)
        sent[i] = jnp.where(first, high, low).astype(jnp.bfloat16)
    across, lines, _, span = terms.shape
    for x in range(across):
        for h in range(lines):
            rows = slice((h * across + x) * span, (h * across + x + 1) * span)
            terms[x, h] = dot(value_grad, weight[rows, :], NT).astype(jnp.bfloat16)


def on_device(
    sublayer_input,
    rotated_queries,
    rotated_keys,
    output_grad,
    value_weight,
    segment_ids,
    label_positions,
):
    bf16, f32 = jnp.bfloat16, jnp.float32
    context = lax.axis_index("ctx")
    mine_y, mine_c = context // (Z * C), context % C
    smem = pl.BlockSpec(memory_space=pltpu.SMEM)
    vmem = pl.BlockSpec(memory_space=pltpu.VMEM)
    params = pltpu.CompilerParams(vmem_limit_bytes=24 * 1024 * 1024)
    column = pl.pallas_call(
        own_kv_kernel,
        out_shape=jax.ShapeDtypeStruct((Z // 4, ROWS, 2 * HD), bf16),
        in_specs=[vmem] * 3,
        out_specs=vmem,
        compiler_params=params,
    )(sublayer_input, value_weight, rotated_keys)
    column, output_grad, rotated_queries = lax.optimization_barrier(
        (column, output_grad, rotated_queries)
    )
    column = lax.all_to_all(column, "ctx", 0, 0, axis_index_groups=COLUMNS)

    own, place = pl.pallas_call(
        own_queries_kernel,
        out_shape=(
            jax.ShapeDtypeStruct((2 * GROUP * ROWS, HD), bf16),
            jax.ShapeDtypeStruct((13 + len(BASES),), jnp.int32),
        ),
        in_specs=[smem] + [vmem] * 4,
        out_specs=(vmem, smem),
        compiler_params=params,
    )(
        context.astype(jnp.int32).reshape(1),
        label_positions[None],
        segment_ids.reshape(-1, HD),
        rotated_queries,
        output_grad,
    )
    across = lax.ppermute(own, "ctx", Y_SWAP)
    beside = lax.ppermute(own, "ctx", C_SWAP)
    plane = Y * C
    column, beside = lax.optimization_barrier((column, beside))
    kv = [
        column,
        along_z(column, 1),
        along_z(column, -1),
        along_z(column[:2], 2),
        along_z(column[2:], -2),
    ]
    corner = lax.ppermute(across, "ctx", C_SWAP)
    operands = [own, across, beside, corner]
    operands += kv
    stat = pltpu.VMEM((GROUP, 8, ROWS), f32)
    all_qd = pltpu.VMEM((plane, 2 * GROUP * ROWS, HD), bf16)
    all_kv = pltpu.VMEM((Z * ROWS, 2 * HD), bf16)
    stats = pl.pallas_call(
        stats_kernel,
        out_shape=jax.ShapeDtypeStruct((3, plane, GROUP, ROWS), f32),
        in_specs=[smem] + [vmem] * PARTS,
        out_specs=vmem,
        scratch_shapes=[all_qd, all_kv, stat, stat, stat],
        compiler_params=params,
    )(place, *operands)
    all_stats = lax.all_gather(stats, "ctx", axis_index_groups=QUADS)
    dq, dq_core, *sums = pl.pallas_call(
        grads_kernel,
        out_shape=[jax.ShapeDtypeStruct((2, ROWS, GROUP * HD), bf16)] * 2
        + [jax.ShapeDtypeStruct((n, ROWS, 2 * HD), bf16) for n in GROUPS],
        in_specs=[smem, vmem] + [vmem] * PARTS,
        out_specs=[vmem] * (2 + len(GROUPS)),
        scratch_shapes=[
            all_qd,
            all_kv,
            pltpu.VMEM((Z, HD, ROWS), bf16),
            pltpu.VMEM((plane, GROUP, ROWS), f32),
            pltpu.VMEM((plane, GROUP, ROWS), f32),
            pltpu.VMEM((TILE, GROUP * ROWS), bf16),
            pltpu.VMEM((TILE, GROUP * ROWS), bf16),
            pltpu.VMEM((HD, GROUP * ROWS), f32),
            pltpu.VMEM((Z * ROWS, 2 * HD), f32),
        ],
        compiler_params=params,
    )(place, all_stats, *operands)

    back = [along_z(part, d) for part, d in zip(sums[1:], (-1, 1, -2, 2))]
    last = jnp.concatenate(back[2:], axis=0)
    column = sums[0].astype(f32) + back[0].astype(f32) + back[1].astype(f32) + last.astype(f32)
    column = lax.all_to_all(column.astype(bf16), "ctx", 0, 0, axis_index_groups=COLUMNS)
    piece = sublayer_input.shape[1] // (Y * Z * C)
    width = value_weight.shape[0] // (2 * X)
    key_grad, kept, sent, terms = pl.pallas_call(
        finish_kernel,
        out_shape=[
            jax.ShapeDtypeStruct((ROWS, HD), bf16),
            jax.ShapeDtypeStruct((Y * Z, piece, HD), bf16),
            jax.ShapeDtypeStruct((Y * Z, piece, HD), bf16),
            jax.ShapeDtypeStruct((X, 2, ROWS, width), bf16),
        ],
        in_specs=[smem] + [vmem] * 3,
        out_specs=[vmem] * 4,
        compiler_params=params,
    )(place, column, sublayer_input, value_weight)
    terms = lax.all_to_all(terms, "mp", 0, 0, axis_index_groups=X_GROUPS)
    terms = jnp.sum(terms.astype(f32), axis=0)
    upper = lax.axis_index("mp") // X == 1
    other = jnp.where(upper, terms[0], terms[1]).astype(bf16)
    other = lax.ppermute(other, "mp", H_SWAP).astype(f32)
    input_grad = (jnp.where(upper, terms[1], terms[0]) + other).astype(bf16)
    near = lax.ppermute(sent, "ctx", C_SWAP)
    term = (kept.astype(f32) + near.astype(f32)).astype(bf16).reshape(Y, Z, piece, HD)
    far = lax.ppermute(jnp.where(mine_y == 0, term[1], term[0]), "ctx", Y_SWAP)
    term = jnp.where(mine_y == 0, term[0], term[1]).astype(f32) + far.astype(f32)
    term = term.astype(bf16)
    from_core = lax.ppermute(dq_core, "ctx", C_SWAP).astype(f32)
    for_across = (dq[1].astype(f32) + from_core[1]).astype(bf16)
    from_across = lax.ppermute(for_across, "ctx", Y_SWAP).astype(f32)
    query_grad = (dq[0].astype(f32) + from_core[0] + from_across).astype(bf16)
    pieces = lax.all_to_all(term, "ctx", 0, 0, axis_index_groups=LINES)
    value_weight_grad = jnp.sum(pieces.astype(f32), axis=0).astype(bf16)
    return (query_grad, key_grad, input_grad, value_weight_grad)


def solution(mesh):
    placed = (
        P("ctx", None),
        P("ctx", "mp"),
        P("ctx", "mp"),
        P("ctx", "mp"),
        P(None, "mp"),
        P(),
        P(),
    )
    return jax.shard_map(
        on_device,
        mesh=mesh,
        in_specs=placed,
        out_specs=(P("ctx", "mp"), P("ctx", "mp"), P("ctx", "mp"), P("ctx", "mp")),
        check_vma=False,
    )
```

```python
import math

import jax
import jax.numpy as jnp
from jax import lax
from jax.experimental import pallas as pl
from jax.experimental.pallas import tpu as pltpu
from jax.sharding import PartitionSpec as P

HEADS = 64
KV_HEADS = 8
GROUP = HEADS // KV_HEADS
HD = 128
ROWS = 128
SCALE = HD ** (-0.5)
POWER = SCALE * math.log2(math.e)
FLOOR = -1e30
HIDDEN = -1e32
Y, Z, C = 2, 16, 2
TILE = 512
BLOCKS = TILE // ROWS
TILES = Z * ROWS // TILE
NT = (((1,), (1,)), ((), ()))
NN = (((1,), (0,)), ((), ()))
TN = (((0,), (0,)), ((), ()))


def at(y, z, c):
    return (y * Z + z) * C + c


Y_SWAP = [(i, i ^ (Z * C)) for i in range(Y * Z * C)]
C_SWAP = [(i, i ^ 1) for i in range(Y * Z * C)]
QUADS = [[at(y, z, c) for y in range(Y) for c in range(C)] for z in range(Z)]
X = 4
X_GROUPS = [[h * X + x for x in range(X)] for h in range(2)]
H_SWAP = [(i, (i + X) % (2 * X)) for i in range(2 * X)]
LINES = [[at(y, z, c) for z in range(Z)] for y in range(Y) for c in range(C)]
COLUMNS = [
    [at(y, z + 4 * k, c) for k in range(Z // 4)]
    for y in range(Y)
    for z in range(4)
    for c in range(C)
]
BASES = [0, 8, 12, 4]
GROUPS = (4, 4, 4, 4)
PARTS = Y * C + len(GROUPS)


def along_z(value, distance, other_distance=None):
    distances = (distance, distance if other_distance is None else other_distance)
    pairs = [
        (at(y, z, c), at((y + distances[c]) % 2, (z + distances[c]) % Z, c))
        for y in range(Y)
        for z in range(Z)
        for c in range(C)
    ]
    return lax.ppermute(value, "ctx", pairs)


def dot(a, b, dims):
    return lax.dot_general(a, b, dims, preferred_element_type=jnp.float32)


def tile_first(place, tile):
    half = TILES // 2
    low = place[4] + 4 * BLOCKS * tile
    high = place[5] + 4 * BLOCKS * (tile - half)
    return jnp.where(tile < half, low, high) * ROWS


def tile_slots(place, tile):
    half = TILES // 2
    residue = jnp.where(tile < half, place[11], 1 - place[11]) - place[12] + Z
    within = lax.rem(tile, half) * (BLOCKS // 2)
    bases = [place[13 + lax.rem(residue + 2 * i, 4)] for i in range(2)]
    return [bases[i % 2] + within + i // 2 for i in range(BLOCKS)]


def slot_rows(slot):
    return pl.ds(pl.multiple_of(slot * ROWS, ROWS), ROWS)


def gather_parts(refs, qd, kv):
    for j in range(Y * C):
        qd[j] = refs[j][...]
    first = 0
    for part in refs[Y * C :]:
        count = part.shape[0]
        for i in range(count):
            kv[(first + i) * ROWS : (first + i + 1) * ROWS, :] = part[i]
        first += count


def doc_start(place, position):
    begin = jnp.zeros_like(position)
    for k in range(6, 9):
        begin = jnp.where(place[k] <= position, jnp.maximum(begin, place[k]), begin)
    return begin


def tile_state(place, j, tile):
    query_first = place[j] * ROWS
    key_first = tile_first(place, tile)
    key_last = key_first + (4 * BLOCKS - 3) * ROWS - 1
    active = (key_first < query_first + ROWS) & (
        key_last >= doc_start(place, query_first)
    )
    return query_first, key_first, active


def tile_mask(place, query_first, key_first):
    row = lax.broadcasted_iota(jnp.int32, (TILE, ROWS), 0)
    key_position = key_first + row + row // ROWS * (3 * ROWS)
    query_position = query_first + lax.broadcasted_iota(jnp.int32, (TILE, ROWS), 1)
    begin = doc_start(place, query_position)
    return (key_position <= query_position) & (key_position >= begin)


def stats_kernel(place, *refs):
    out, qd, kv, top, total, inner = refs[PARTS:]
    gather_parts(refs[:PARTS], qd, kv)

    def query_block(j, _):
        top[...] = jnp.full(top.shape, FLOOR, jnp.float32)
        total[...] = jnp.zeros(total.shape, jnp.float32)
        inner[...] = jnp.zeros(inner.shape, jnp.float32)

        def key_tile(tile, _):
            query_first, key_first, active = tile_state(place, j, tile)

            @pl.when(active)
            def _():
                mask = tile_mask(place, query_first, key_first)
                slots = tile_slots(place, tile)
                spans = [slot_rows(slot) for slot in slots]
                keys = jnp.concatenate([kv[rows, :HD] for rows in spans], axis=0)
                values = jnp.concatenate([kv[rows, HD:] for rows in spans], axis=0)
                for pair in range(GROUP // 2):
                    span = pl.ds(pair * 2 * ROWS, 2 * ROWS)
                    grad_span = pl.ds((GROUP + pair * 2) * ROWS, 2 * ROWS)
                    scores = dot(keys, qd[j, span, :], NT)
                    grad_probs = dot(values, qd[j, grad_span, :], NT)
                    for i in range(2):
                        head = 2 * pair + i
                        lanes = slice(i * ROWS, (i + 1) * ROWS)
                        s = jnp.where(mask, scores[:, lanes], HIDDEN)
                        s = s.reshape(TILE // 8, 8, ROWS)
                        g = grad_probs[:, lanes].reshape(TILE // 8, 8, ROWS)
                        old = top[head]
                        new = jnp.maximum(old, jnp.max(s, axis=0))
                        factor = jnp.exp2((old - new) * POWER)
                        p = jnp.exp2((s - new[None]) * POWER)
                        total[head] = total[head] * factor + jnp.sum(p, axis=0)
                        inner[head] = inner[head] * factor + jnp.sum(p * g, axis=0)
                        top[head] = new

            return 0

        lax.fori_loop(0, TILES, key_tile, 0)
        tops = top[...]
        best = jnp.max(tops, axis=1)
        weight = jnp.exp2((tops - best[:, None, :]) * POWER)
        out[0, j] = best
        out[1, j] = jnp.sum(total[...] * weight, axis=1)
        out[2, j] = jnp.sum(inner[...] * weight, axis=1)
        return 0

    lax.fori_loop(0, Y * C, query_block, 0)


def grads_kernel(place, stats, *refs):
    dq, dq_core = refs[PARTS : PARTS + 2]
    sums, scratch = refs[PARTS + 2 : PARTS + 2 + len(GROUPS)], refs[PARTS + 2 + len(GROUPS) :]
    qd, kv, kt, log_total, delta, probs, grad_scores, dqt, dkv_sum = scratch
    gather_parts(refs[:PARTS], qd, kv)
    for slot in range(Z):
        rows = slice(slot * ROWS, (slot + 1) * ROWS)
        kt[slot] = kv[rows, :HD].T
    mine_y, mine_c = place[9], place[10]
    for j in range(Y * C):
        parts = []
        for r in range(Y * C):
            slot = 2 * (mine_y ^ (r & 1)) + (mine_c ^ (r >> 1))
            parts.append([stats[slot, k, j ^ r] for k in range(3)])
        best = parts[0][0]
        for part in parts[1:]:
            best = jnp.maximum(best, part[0])
        total = jnp.zeros_like(best)
        inner = jnp.zeros_like(best)
        for part in parts:
            weight = jnp.exp2((part[0] - best) * POWER)
            total += part[1] * weight
            inner += part[2] * weight
        log_total[j] = best * POWER + jnp.log(total) * math.log2(math.e)
        delta[j] = inner / total
    dkv_sum[...] = jnp.zeros(dkv_sum.shape, jnp.float32)

    def query_block(j, _):
        dqt[...] = jnp.zeros(dqt.shape, jnp.float32)

        def key_tile(tile, _):
            query_first, key_first, active = tile_state(place, j, tile)

            @pl.when(active)
            def _():
                mask = tile_mask(place, query_first, key_first)
                slots = tile_slots(place, tile)
                spans = [slot_rows(slot) for slot in slots]
                keys = jnp.concatenate([kv[rows, :HD] for rows in spans], axis=0)
                values = jnp.concatenate([kv[rows, HD:] for rows in spans], axis=0)
                for pair in range(GROUP // 2):
                    span = pl.ds(pair * 2 * ROWS, 2 * ROWS)
                    grad_span = pl.ds((GROUP + pair * 2) * ROWS, 2 * ROWS)
                    scores = dot(keys, qd[j, span, :], NT)
                    grads = dot(values, qd[j, grad_span, :], NT)
                    for i in range(2):
                        head = 2 * pair + i
                        lanes = slice(i * ROWS, (i + 1) * ROWS)
                        whole = slice(head * ROWS, (head + 1) * ROWS)
                        x = scores[:, lanes] * POWER - log_total[j, pl.ds(head, 1), :]
                        p = jnp.exp2(jnp.where(mask, x, FLOOR))
                        probs[:, whole] = p.astype(jnp.bfloat16)
                        d = p * (grads[:, lanes] - delta[j, pl.ds(head, 1), :])
                        grad_scores[:, whole] = d.astype(jnp.bfloat16)
                weights = grad_scores[...]
                keys_t = jnp.concatenate([kt[slot] for slot in slots], axis=1)
                dqt[...] += dot(keys_t, weights, NN)
                key_term = dot(weights, qd[j, pl.ds(0, GROUP * ROWS), :], NN)
                value_term = dot(probs[...], qd[j, pl.ds(GROUP * ROWS, GROUP * ROWS), :], NN)
                for i, rows in enumerate(spans):
                    dkv_sum[rows, :HD] += key_term[i * ROWS : (i + 1) * ROWS]
                    dkv_sum[rows, HD:] += value_term[i * ROWS : (i + 1) * ROWS]

            return 0

        lax.fori_loop(0, TILES, key_tile, 0)
        for half, place_of in enumerate((dq, dq_core)):

            @pl.when(j // 2 == half)
            def _():
                for head in range(GROUP):
                    lanes = slice(head * ROWS, (head + 1) * ROWS)
                    turned = dqt[:, lanes].T * SCALE
                    place_of[lax.rem(j, 2), :, lanes] = turned.astype(jnp.bfloat16)

        return 0

    lax.fori_loop(0, Y * C, query_block, 0)
    slot = 0
    for part in sums:
        for i in range(part.shape[0]):
            rows = slice(slot * ROWS, (slot + 1) * ROWS)
            part[i, :, :HD] = (dkv_sum[rows, :HD] * SCALE).astype(jnp.bfloat16)
            part[i, :, HD:] = dkv_sum[rows, HD:].astype(jnp.bfloat16)
            slot += 1


def own_kv_kernel(inputs, weight, keys, out):
    values = dot(inputs[...], weight[...], NN).astype(jnp.bfloat16)
    for k in range(out.shape[0]):
        out[k, :, :HD] = keys[...]
        out[k, :, HD:] = values


def own_queries_kernel(index, labels, segments, queries, grads, out, place):
    context = index[0]
    y, z, c = context // (Z * C), lax.rem(context // C, Z), lax.rem(context, C)
    side = lax.rem(y + z, 2)
    for j in range(Y * C):
        place[j] = at(y ^ (j & 1), z, c ^ (j >> 1))
    place[4] = 2 * side + c
    place[5] = 2 * Z + 2 * (1 - side) + c
    for k in range(1, 4):
        before = jnp.where(segments[...] < k, 1.0, 0.0).astype(jnp.float32)
        place[5 + k] = jnp.sum(before).astype(jnp.int32)
    for i, value in enumerate((y, c, side, z)):
        place[9 + i] = value
    for i, base in enumerate(BASES):
        place[13 + i] = base
    position = context * ROWS + lax.broadcasted_iota(
        jnp.int32, (ROWS, labels.shape[1]), 0
    )
    labelled = jnp.where(position == labels[...], 3.0, 0.0).astype(jnp.float32)
    weight = 1.0 + jnp.max(labelled, axis=1, keepdims=True)
    for head in range(GROUP):
        lanes = slice(head * HD, (head + 1) * HD)
        out[head * ROWS : (head + 1) * ROWS] = queries[:, lanes]
        weighted = grads[:, lanes].astype(jnp.float32) * weight
        out[(GROUP + head) * ROWS : (GROUP + head + 1) * ROWS] = weighted.astype(jnp.bfloat16)


def finish_kernel(place, parts, inputs, weight, key_grad, kept, sent, terms):
    summed = parts[0].astype(jnp.float32)
    for i in range(1, parts.shape[0]):
        summed += parts[i].astype(jnp.float32)
    summed = summed.astype(jnp.bfloat16)
    key_grad[...] = summed[:, :HD]
    value_grad = summed[:, HD:]
    total = dot(value_grad, inputs[...], TN)
    width = kept.shape[1]
    first = place[10] == 0
    for i in range(kept.shape[0]):
        turned = total[:, i * C * width : (i + 1) * C * width].T
        low, high = turned[:width], turned[width:]
        kept[i] = jnp.where(first, low, high).astype(jnp.bfloat16)
        sent[i] = jnp.where(first, high, low).astype(jnp.bfloat16)
    across, lines, _, span = terms.shape
    for x in range(across):
        for h in range(lines):
            rows = slice((h * across + x) * span, (h * across + x + 1) * span)
            terms[x, h] = dot(value_grad, weight[rows, :], NT).astype(jnp.bfloat16)


def on_device(
    sublayer_input,
    rotated_queries,
    rotated_keys,
    output_grad,
    value_weight,
    segment_ids,
    label_positions,
):
    bf16, f32 = jnp.bfloat16, jnp.float32
    context = lax.axis_index("ctx")
    mine_y, mine_c = context // (Z * C), context % C
    smem = pl.BlockSpec(memory_space=pltpu.SMEM)
    vmem = pl.BlockSpec(memory_space=pltpu.VMEM)
    params = pltpu.CompilerParams(vmem_limit_bytes=24 * 1024 * 1024)
    column = pl.pallas_call(
        own_kv_kernel,
        out_shape=jax.ShapeDtypeStruct((Z // 4, ROWS, 2 * HD), bf16),
        in_specs=[vmem] * 3,
        out_specs=vmem,
        compiler_params=params,
    )(sublayer_input, value_weight, rotated_keys)
    column, output_grad, rotated_queries = lax.optimization_barrier(
        (column, output_grad, rotated_queries)
    )
    column = lax.all_to_all(column, "ctx", 0, 0, axis_index_groups=COLUMNS)

    own, place = pl.pallas_call(
        own_queries_kernel,
        out_shape=(
            jax.ShapeDtypeStruct((2 * GROUP * ROWS, HD), bf16),
            jax.ShapeDtypeStruct((13 + len(BASES),), jnp.int32),
        ),
        in_specs=[smem] + [vmem] * 4,
        out_specs=(vmem, smem),
        compiler_params=params,
    )(
        context.astype(jnp.int32).reshape(1),
        label_positions[None],
        segment_ids.reshape(-1, HD),
        rotated_queries,
        output_grad,
    )
    across = lax.ppermute(own, "ctx", Y_SWAP)
    beside = lax.ppermute(own, "ctx", C_SWAP)
    plane = Y * C
    column, beside = lax.optimization_barrier((column, beside))
    kv = [
        column,
        along_z(column, 1),
        along_z(column, -1),
        along_z(column, 2, -2),
    ]
    corner = lax.ppermute(across, "ctx", C_SWAP)
    operands = [own, across, beside, corner]
    operands += kv
    stat = pltpu.VMEM((GROUP, 8, ROWS), f32)
    all_qd = pltpu.VMEM((plane, 2 * GROUP * ROWS, HD), bf16)
    all_kv = pltpu.VMEM((Z * ROWS, 2 * HD), bf16)
    stats = pl.pallas_call(
        stats_kernel,
        out_shape=jax.ShapeDtypeStruct((3, plane, GROUP, ROWS), f32),
        in_specs=[smem] + [vmem] * PARTS,
        out_specs=vmem,
        scratch_shapes=[all_qd, all_kv, stat, stat, stat],
        compiler_params=params,
    )(place, *operands)
    all_stats = lax.all_gather(stats, "ctx", axis_index_groups=QUADS)
    dq, dq_core, *sums = pl.pallas_call(
        grads_kernel,
        out_shape=[jax.ShapeDtypeStruct((2, ROWS, GROUP * HD), bf16)] * 2
        + [jax.ShapeDtypeStruct((n, ROWS, 2 * HD), bf16) for n in GROUPS],
        in_specs=[smem, vmem] + [vmem] * PARTS,
        out_specs=[vmem] * (2 + len(GROUPS)),
        scratch_shapes=[
            all_qd,
            all_kv,
            pltpu.VMEM((Z, HD, ROWS), bf16),
            pltpu.VMEM((plane, GROUP, ROWS), f32),
            pltpu.VMEM((plane, GROUP, ROWS), f32),
            pltpu.VMEM((TILE, GROUP * ROWS), bf16),
            pltpu.VMEM((TILE, GROUP * ROWS), bf16),
            pltpu.VMEM((HD, GROUP * ROWS), f32),
            pltpu.VMEM((Z * ROWS, 2 * HD), f32),
        ],
        compiler_params=params,
    )(place, all_stats, *operands)

    back = [along_z(sums[1], -1), along_z(sums[2], 1), along_z(sums[3], -2, 2)]
    column = sums[0].astype(f32)
    for part in back:
        column += part.astype(f32)
    column = lax.all_to_all(column.astype(bf16), "ctx", 0, 0, axis_index_groups=COLUMNS)
    piece = sublayer_input.shape[1] // (Y * Z * C)
    width = value_weight.shape[0] // (2 * X)
    key_grad, kept, sent, terms = pl.pallas_call(
        finish_kernel,
        out_shape=[
            jax.ShapeDtypeStruct((ROWS, HD), bf16),
            jax.ShapeDtypeStruct((Y * Z, piece, HD), bf16),
            jax.ShapeDtypeStruct((Y * Z, piece, HD), bf16),
            jax.ShapeDtypeStruct((X, 2, ROWS, width), bf16),
        ],
        in_specs=[smem] + [vmem] * 3,
        out_specs=[vmem] * 4,
        compiler_params=params,
    )(place, column, sublayer_input, value_weight)
    terms = lax.all_to_all(terms, "mp", 0, 0, axis_index_groups=X_GROUPS)
    terms = jnp.sum(terms.astype(f32), axis=0)
    upper = lax.axis_index("mp") // X == 1
    other = jnp.where(upper, terms[0], terms[1]).astype(bf16)
    other = lax.ppermute(other, "mp", H_SWAP).astype(f32)
    input_grad = (jnp.where(upper, terms[1], terms[0]) + other).astype(bf16)
    near = lax.ppermute(sent, "ctx", C_SWAP)
    term = (kept.astype(f32) + near.astype(f32)).astype(bf16).reshape(Y, Z, piece, HD)
    far = lax.ppermute(jnp.where(mine_y == 0, term[1], term[0]), "ctx", Y_SWAP)
    term = jnp.where(mine_y == 0, term[0], term[1]).astype(f32) + far.astype(f32)
    term = term.astype(bf16)
    from_core = lax.ppermute(dq_core, "ctx", C_SWAP).astype(f32)
    for_across = (dq[1].astype(f32) + from_core[1]).astype(bf16)
    from_across = lax.ppermute(for_across, "ctx", Y_SWAP).astype(f32)
    query_grad = (dq[0].astype(f32) + from_core[0] + from_across).astype(bf16)
    pieces = lax.all_to_all(term, "ctx", 0, 0, axis_index_groups=LINES)
    value_weight_grad = jnp.sum(pieces.astype(f32), axis=0).astype(bf16)
    return (query_grad, key_grad, input_grad, value_weight_grad)


def solution(mesh):
    placed = (
        P("ctx", None),
        P("ctx", "mp"),
        P("ctx", "mp"),
        P("ctx", "mp"),
        P(None, "mp"),
        P(),
        P(),
    )
    return jax.shard_map(
        on_device,
        mesh=mesh,
        in_specs=placed,
        out_specs=(P("ctx", "mp"), P("ctx", "mp"), P("ctx", "mp"), P("ctx", "mp")),
        check_vma=False,
    )
```

```python
import math

import jax
import jax.numpy as jnp
from jax import lax
from jax.experimental import pallas as pl
from jax.experimental.pallas import tpu as pltpu
from jax.sharding import PartitionSpec as P

HEADS = 64
KV_HEADS = 8
GROUP = HEADS // KV_HEADS
HD = 128
ROWS = 128
SCALE = HD ** (-0.5)
POWER = SCALE * math.log2(math.e)
FLOOR = -1e30
HIDDEN = -1e32
Y, Z, C = 2, 16, 2
TILE = 512
BLOCKS = TILE // ROWS
TILES = Z * ROWS // TILE
NT = (((1,), (1,)), ((), ()))
NN = (((1,), (0,)), ((), ()))
TN = (((0,), (0,)), ((), ()))


def at(y, z, c):
    return (y * Z + z) * C + c


Y_SWAP = [(i, i ^ (Z * C)) for i in range(Y * Z * C)]
C_SWAP = [(i, i ^ 1) for i in range(Y * Z * C)]
QUADS = [[at(y, z, c) for y in range(Y) for c in range(C)] for z in range(Z)]
X = 4
X_GROUPS = [[h * X + x for x in range(X)] for h in range(2)]
H_SWAP = [(i, (i + X) % (2 * X)) for i in range(2 * X)]
LINES = [[at(y, z, c) for z in range(Z)] for y in range(Y) for c in range(C)]
COLUMNS = [
    [at(y, z + 4 * k, c) for k in range(Z // 4)]
    for y in range(Y)
    for z in range(4)
    for c in range(C)
]
BASES = [0, 8, 12, 4]
GROUPS = (4, 4, 4, 2, 2)
PARTS = Y * C + len(GROUPS)


def along_z(value, distance):
    pairs = [
        (at(y, z, c), at((y + distance) % 2, (z + distance) % Z, c))
        for y in range(Y)
        for z in range(Z)
        for c in range(C)
    ]
    return lax.ppermute(value, "ctx", pairs)


def dot(a, b, dims):
    return lax.dot_general(a, b, dims, preferred_element_type=jnp.float32)


def tile_first(place, tile):
    half = TILES // 2
    low = place[4] + 4 * BLOCKS * tile
    high = place[5] + 4 * BLOCKS * (tile - half)
    return jnp.where(tile < half, low, high) * ROWS


def tile_slots(place, tile):
    half = TILES // 2
    residue = jnp.where(tile < half, place[11], 1 - place[11]) - place[12] + Z
    within = lax.rem(tile, half) * (BLOCKS // 2)
    bases = [place[13 + lax.rem(residue + 2 * i, 4)] for i in range(2)]
    return [bases[i % 2] + within + i // 2 for i in range(BLOCKS)]


def slot_rows(slot):
    return pl.ds(pl.multiple_of(slot * ROWS, ROWS), ROWS)


def gather_parts(refs, qd, kv):
    for j in range(Y * C):
        qd[j] = refs[j][...]
    first = 0
    for part in refs[Y * C :]:
        count = part.shape[0]
        for i in range(count):
            kv[(first + i) * ROWS : (first + i + 1) * ROWS, :] = part[i]
        first += count


def doc_start(place, position):
    begin = jnp.zeros_like(position)
    for k in range(6, 9):
        begin = jnp.where(place[k] <= position, jnp.maximum(begin, place[k]), begin)
    return begin


def tile_state(place, j, tile):
    query_first = place[j] * ROWS
    key_first = tile_first(place, tile)
    key_last = key_first + (4 * BLOCKS - 3) * ROWS - 1
    active = (key_first < query_first + ROWS) & (
        key_last >= doc_start(place, query_first)
    )
    return query_first, key_first, active


def tile_mask(place, query_first, key_first):
    row = lax.broadcasted_iota(jnp.int32, (TILE, ROWS), 0)
    key_position = key_first + row + row // ROWS * (3 * ROWS)
    query_position = query_first + lax.broadcasted_iota(jnp.int32, (TILE, ROWS), 1)
    begin = doc_start(place, query_position)
    return (key_position <= query_position) & (key_position >= begin)


def stats_kernel(place, *refs):
    out, qd, kv, top, total, inner = refs[PARTS:]
    gather_parts(refs[:PARTS], qd, kv)

    def query_block(j, _):
        top[...] = jnp.full(top.shape, FLOOR, jnp.float32)
        total[...] = jnp.zeros(total.shape, jnp.float32)
        inner[...] = jnp.zeros(inner.shape, jnp.float32)

        def key_tile(tile, _):
            query_first, key_first, active = tile_state(place, j, tile)

            @pl.when(active)
            def _():
                mask = tile_mask(place, query_first, key_first)
                slots = tile_slots(place, tile)
                spans = [slot_rows(slot) for slot in slots]
                keys = jnp.concatenate([kv[rows, :HD] for rows in spans], axis=0)
                values = jnp.concatenate([kv[rows, HD:] for rows in spans], axis=0)
                for pair in range(GROUP // 2):
                    span = pl.ds(pair * 2 * ROWS, 2 * ROWS)
                    grad_span = pl.ds((GROUP + pair * 2) * ROWS, 2 * ROWS)
                    scores = dot(keys, qd[j, span, :], NT)
                    grad_probs = dot(values, qd[j, grad_span, :], NT)
                    for i in range(2):
                        head = 2 * pair + i
                        lanes = slice(i * ROWS, (i + 1) * ROWS)
                        s = jnp.where(mask, scores[:, lanes], HIDDEN)
                        s = s.reshape(TILE // 8, 8, ROWS)
                        g = grad_probs[:, lanes].reshape(TILE // 8, 8, ROWS)
                        old = top[head]
                        new = jnp.maximum(old, jnp.max(s, axis=0))
                        factor = jnp.exp2((old - new) * POWER)
                        p = jnp.exp2((s - new[None]) * POWER)
                        total[head] = total[head] * factor + jnp.sum(p, axis=0)
                        inner[head] = inner[head] * factor + jnp.sum(p * g, axis=0)
                        top[head] = new

            return 0

        lax.fori_loop(0, TILES, key_tile, 0)
        tops = top[...]
        best = jnp.max(tops, axis=1)
        weight = jnp.exp2((tops - best[:, None, :]) * POWER)
        out[0, j] = best
        out[1, j] = jnp.sum(total[...] * weight, axis=1)
        out[2, j] = jnp.sum(inner[...] * weight, axis=1)
        return 0

    lax.fori_loop(0, Y * C, query_block, 0)


def grads_kernel(place, stats, *refs):
    dq, dq_core = refs[PARTS : PARTS + 2]
    sums, scratch = refs[PARTS + 2 : PARTS + 2 + len(GROUPS)], refs[PARTS + 2 + len(GROUPS) :]
    qd, kv, kt, log_total, delta, probs, grad_scores, dqt, dkv_sum = scratch
    gather_parts(refs[:PARTS], qd, kv)
    for slot in range(Z):
        rows = slice(slot * ROWS, (slot + 1) * ROWS)
        kt[slot] = kv[rows, :HD].T
    mine_y, mine_c = place[9], place[10]
    for j in range(Y * C):
        parts = []
        for r in range(Y * C):
            slot = 2 * (mine_y ^ (r & 1)) + (mine_c ^ (r >> 1))
            parts.append([stats[slot, k, j ^ r] for k in range(3)])
        best = parts[0][0]
        for part in parts[1:]:
            best = jnp.maximum(best, part[0])
        total = jnp.zeros_like(best)
        inner = jnp.zeros_like(best)
        for part in parts:
            weight = jnp.exp2((part[0] - best) * POWER)
            total += part[1] * weight
            inner += part[2] * weight
        log_total[j] = best * POWER + jnp.log(total) * math.log2(math.e)
        delta[j] = inner / total
    dkv_sum[...] = jnp.zeros(dkv_sum.shape, jnp.float32)

    def query_block(j, _):
        dqt[...] = jnp.zeros(dqt.shape, jnp.float32)

        def key_tile(tile, _):
            query_first, key_first, active = tile_state(place, j, tile)

            @pl.when(active)
            def _():
                mask = tile_mask(place, query_first, key_first)
                slots = tile_slots(place, tile)
                spans = [slot_rows(slot) for slot in slots]
                keys = jnp.concatenate([kv[rows, :HD] for rows in spans], axis=0)
                values = jnp.concatenate([kv[rows, HD:] for rows in spans], axis=0)
                for pair in range(GROUP // 2):
                    span = pl.ds(pair * 2 * ROWS, 2 * ROWS)
                    grad_span = pl.ds((GROUP + pair * 2) * ROWS, 2 * ROWS)
                    scores = dot(keys, qd[j, span, :], NT)
                    grads = dot(values, qd[j, grad_span, :], NT)
                    for i in range(2):
                        head = 2 * pair + i
                        lanes = slice(i * ROWS, (i + 1) * ROWS)
                        whole = slice(head * ROWS, (head + 1) * ROWS)
                        x = scores[:, lanes] * POWER - log_total[j, pl.ds(head, 1), :]
                        p = jnp.exp2(jnp.where(mask, x, FLOOR))
                        probs[:, whole] = p.astype(jnp.bfloat16)
                        d = p * (grads[:, lanes] - delta[j, pl.ds(head, 1), :])
                        grad_scores[:, whole] = d.astype(jnp.bfloat16)
                weights = grad_scores[...]
                keys_t = jnp.concatenate([kt[slot] for slot in slots], axis=1)
                dqt[...] += dot(keys_t, weights, NN)
                key_term = dot(weights, qd[j, pl.ds(0, GROUP * ROWS), :], NN)
                value_term = dot(probs[...], qd[j, pl.ds(GROUP * ROWS, GROUP * ROWS), :], NN)
                for i, rows in enumerate(spans):
                    dkv_sum[rows, :HD] += key_term[i * ROWS : (i + 1) * ROWS]
                    dkv_sum[rows, HD:] += value_term[i * ROWS : (i + 1) * ROWS]

            return 0

        lax.fori_loop(0, TILES, key_tile, 0)
        for half, place_of in enumerate((dq, dq_core)):

            @pl.when(j // 2 == half)
            def _():
                for head in range(GROUP):
                    lanes = slice(head * ROWS, (head + 1) * ROWS)
                    turned = dqt[:, lanes].T * SCALE
                    place_of[lax.rem(j, 2), :, lanes] = turned.astype(jnp.bfloat16)

        return 0

    lax.fori_loop(0, Y * C, query_block, 0)
    slot = 0
    for part in sums:
        for i in range(part.shape[0]):
            rows = slice(slot * ROWS, (slot + 1) * ROWS)
            part[i, :, :HD] = (dkv_sum[rows, :HD] * SCALE).astype(jnp.bfloat16)
            part[i, :, HD:] = dkv_sum[rows, HD:].astype(jnp.bfloat16)
            slot += 1


def own_kv_kernel(inputs, weight, keys, out):
    values = dot(inputs[...], weight[...], NN).astype(jnp.bfloat16)
    for k in range(out.shape[0]):
        out[k, :, :HD] = keys[...]
        out[k, :, HD:] = values


def own_queries_kernel(index, labels, segments, queries, grads, out, place):
    context = index[0]
    y, z, c = context // (Z * C), lax.rem(context // C, Z), lax.rem(context, C)
    side = lax.rem(y + z, 2)
    for j in range(Y * C):
        place[j] = at(y ^ (j & 1), z, c ^ (j >> 1))
    place[4] = 2 * side + c
    place[5] = 2 * Z + 2 * (1 - side) + c
    for k in range(1, 4):
        before = jnp.where(segments[...] < k, 1.0, 0.0).astype(jnp.float32)
        place[5 + k] = jnp.sum(before).astype(jnp.int32)
    for i, value in enumerate((y, c, side, z)):
        place[9 + i] = value
    for i, base in enumerate(BASES):
        place[13 + i] = base
    position = context * ROWS + lax.broadcasted_iota(
        jnp.int32, (ROWS, labels.shape[1]), 0
    )
    labelled = jnp.where(position == labels[...], 3.0, 0.0).astype(jnp.float32)
    weight = 1.0 + jnp.max(labelled, axis=1, keepdims=True)
    for head in range(GROUP):
        lanes = slice(head * HD, (head + 1) * HD)
        out[head * ROWS : (head + 1) * ROWS] = queries[:, lanes]
        weighted = grads[:, lanes].astype(jnp.float32) * weight
        out[(GROUP + head) * ROWS : (GROUP + head + 1) * ROWS] = weighted.astype(jnp.bfloat16)


def finish_kernel(place, parts, inputs, weight, key_grad, kept, sent, terms):
    summed = parts[0].astype(jnp.float32)
    for i in range(1, parts.shape[0]):
        summed += parts[i].astype(jnp.float32)
    summed = summed.astype(jnp.bfloat16)
    key_grad[...] = summed[:, :HD]
    value_grad = summed[:, HD:]
    total = dot(value_grad, inputs[...], TN)
    width = kept.shape[1]
    first = place[10] == 0
    for i in range(kept.shape[0]):
        turned = total[:, i * C * width : (i + 1) * C * width].T
        low, high = turned[:width], turned[width:]
        kept[i] = jnp.where(first, low, high).astype(jnp.bfloat16)
        sent[i] = jnp.where(first, high, low).astype(jnp.bfloat16)
    across, lines, _, span = terms.shape
    for x in range(across):
        for h in range(lines):
            rows = slice((h * across + x) * span, (h * across + x + 1) * span)
            terms[x, h] = dot(value_grad, weight[rows, :], NT).astype(jnp.bfloat16)


def on_device(
    sublayer_input,
    rotated_queries,
    rotated_keys,
    output_grad,
    value_weight,
    segment_ids,
    label_positions,
):
    bf16, f32 = jnp.bfloat16, jnp.float32
    context = lax.axis_index("ctx")
    mine_y, mine_c = context // (Z * C), context % C
    smem = pl.BlockSpec(memory_space=pltpu.SMEM)
    vmem = pl.BlockSpec(memory_space=pltpu.VMEM)
    params = pltpu.CompilerParams(vmem_limit_bytes=24 * 1024 * 1024)
    column = pl.pallas_call(
        own_kv_kernel,
        out_shape=jax.ShapeDtypeStruct((Z // 4, ROWS, 2 * HD), bf16),
        in_specs=[vmem] * 3,
        out_specs=vmem,
        compiler_params=params,
    )(sublayer_input, value_weight, rotated_keys)
    column, output_grad, rotated_queries = lax.optimization_barrier(
        (column, output_grad, rotated_queries)
    )
    column = lax.all_to_all(column, "ctx", 0, 0, axis_index_groups=COLUMNS)

    own, place = pl.pallas_call(
        own_queries_kernel,
        out_shape=(
            jax.ShapeDtypeStruct((2 * GROUP * ROWS, HD), bf16),
            jax.ShapeDtypeStruct((13 + len(BASES),), jnp.int32),
        ),
        in_specs=[smem] + [vmem] * 4,
        out_specs=(vmem, smem),
        compiler_params=params,
    )(
        context.astype(jnp.int32).reshape(1),
        label_positions[None],
        segment_ids.reshape(-1, HD),
        rotated_queries,
        output_grad,
    )
    across = lax.ppermute(own, "ctx", Y_SWAP)
    beside = lax.ppermute(own, "ctx", C_SWAP)
    plane = Y * C
    column, beside = lax.optimization_barrier((column, beside))
    kv = [
        column,
        along_z(column, 1),
        along_z(column, -1),
        along_z(column[:2], 2),
        along_z(column[2:], -2),
    ]
    across, kv = lax.optimization_barrier((across, kv))
    corner = lax.ppermute(across, "ctx", C_SWAP)
    operands = [own, across, beside, corner]
    operands += kv
    stat = pltpu.VMEM((GROUP, 8, ROWS), f32)
    all_qd = pltpu.VMEM((plane, 2 * GROUP * ROWS, HD), bf16)
    all_kv = pltpu.VMEM((Z * ROWS, 2 * HD), bf16)
    stats = pl.pallas_call(
        stats_kernel,
        out_shape=jax.ShapeDtypeStruct((3, plane, GROUP, ROWS), f32),
        in_specs=[smem] + [vmem] * PARTS,
        out_specs=vmem,
        scratch_shapes=[all_qd, all_kv, stat, stat, stat],
        compiler_params=params,
    )(place, *operands)
    all_stats = lax.all_gather(stats, "ctx", axis_index_groups=QUADS)
    dq, dq_core, *sums = pl.pallas_call(
        grads_kernel,
        out_shape=[jax.ShapeDtypeStruct((2, ROWS, GROUP * HD), bf16)] * 2
        + [jax.ShapeDtypeStruct((n, ROWS, 2 * HD), bf16) for n in GROUPS],
        in_specs=[smem, vmem] + [vmem] * PARTS,
        out_specs=[vmem] * (2 + len(GROUPS)),
        scratch_shapes=[
            all_qd,
            all_kv,
            pltpu.VMEM((Z, HD, ROWS), bf16),
            pltpu.VMEM((plane, GROUP, ROWS), f32),
            pltpu.VMEM((plane, GROUP, ROWS), f32),
            pltpu.VMEM((TILE, GROUP * ROWS), bf16),
            pltpu.VMEM((TILE, GROUP * ROWS), bf16),
            pltpu.VMEM((HD, GROUP * ROWS), f32),
            pltpu.VMEM((Z * ROWS, 2 * HD), f32),
        ],
        compiler_params=params,
    )(place, all_stats, *operands)

    back = [along_z(part, d) for part, d in zip(sums[1:], (-1, 1, -2, 2))]
    last = jnp.concatenate(back[2:], axis=0)
    column = sums[0].astype(f32) + back[0].astype(f32) + back[1].astype(f32) + last.astype(f32)
    column = lax.all_to_all(column.astype(bf16), "ctx", 0, 0, axis_index_groups=COLUMNS)
    piece = sublayer_input.shape[1] // (Y * Z * C)
    width = value_weight.shape[0] // (2 * X)
    key_grad, kept, sent, terms = pl.pallas_call(
        finish_kernel,
        out_shape=[
            jax.ShapeDtypeStruct((ROWS, HD), bf16),
            jax.ShapeDtypeStruct((Y * Z, piece, HD), bf16),
            jax.ShapeDtypeStruct((Y * Z, piece, HD), bf16),
            jax.ShapeDtypeStruct((X, 2, ROWS, width), bf16),
        ],
        in_specs=[smem] + [vmem] * 3,
        out_specs=[vmem] * 4,
        compiler_params=params,
    )(place, column, sublayer_input, value_weight)
    terms = lax.all_to_all(terms, "mp", 0, 0, axis_index_groups=X_GROUPS)
    terms = jnp.sum(terms.astype(f32), axis=0)
    upper = lax.axis_index("mp") // X == 1
    other = jnp.where(upper, terms[0], terms[1]).astype(bf16)
    other = lax.ppermute(other, "mp", H_SWAP).astype(f32)
    input_grad = (jnp.where(upper, terms[1], terms[0]) + other).astype(bf16)
    near = lax.ppermute(sent, "ctx", C_SWAP)
    term = (kept.astype(f32) + near.astype(f32)).astype(bf16).reshape(Y, Z, piece, HD)
    far = lax.ppermute(jnp.where(mine_y == 0, term[1], term[0]), "ctx", Y_SWAP)
    term = jnp.where(mine_y == 0, term[0], term[1]).astype(f32) + far.astype(f32)
    term = term.astype(bf16)
    from_core = lax.ppermute(dq_core, "ctx", C_SWAP).astype(f32)
    for_across = (dq[1].astype(f32) + from_core[1]).astype(bf16)
    from_across = lax.ppermute(for_across, "ctx", Y_SWAP).astype(f32)
    query_grad = (dq[0].astype(f32) + from_core[0] + from_across).astype(bf16)
    pieces = lax.all_to_all(term, "ctx", 0, 0, axis_index_groups=LINES)
    value_weight_grad = jnp.sum(pieces.astype(f32), axis=0).astype(bf16)
    return (query_grad, key_grad, input_grad, value_weight_grad)


def solution(mesh):
    placed = (
        P("ctx", None),
        P("ctx", "mp"),
        P("ctx", "mp"),
        P("ctx", "mp"),
        P(None, "mp"),
        P(),
        P(),
    )
    return jax.shard_map(
        on_device,
        mesh=mesh,
        in_specs=placed,
        out_specs=(P("ctx", "mp"), P("ctx", "mp"), P("ctx", "mp"), P("ctx", "mp")),
        check_vma=False,
    )
```

```python
import math

import jax
import jax.numpy as jnp
from jax import lax
from jax.experimental import pallas as pl
from jax.experimental.pallas import tpu as pltpu
from jax.sharding import PartitionSpec as P

HEADS = 64
KV_HEADS = 8
GROUP = HEADS // KV_HEADS
HD = 128
ROWS = 128
SCALE = HD ** (-0.5)
POWER = SCALE * math.log2(math.e)
FLOOR = -1e30
HIDDEN = -1e32
Y, Z, C = 2, 16, 2
TILE = 512
BLOCKS = TILE // ROWS
TILES = Z * ROWS // TILE
NT = (((1,), (1,)), ((), ()))
NN = (((1,), (0,)), ((), ()))
TN = (((0,), (0,)), ((), ()))


def at(y, z, c):
    return (y * Z + z) * C + c


Y_SWAP = [(i, i ^ (Z * C)) for i in range(Y * Z * C)]
C_SWAP = [(i, i ^ 1) for i in range(Y * Z * C)]
QUADS = [[at(y, z, c) for y in range(Y) for c in range(C)] for z in range(Z)]
X = 4
X_GROUPS = [[h * X + x for x in range(X)] for h in range(2)]
H_SWAP = [(i, (i + X) % (2 * X)) for i in range(2 * X)]
LINES = [[at(y, z, c) for z in range(Z)] for y in range(Y) for c in range(C)]
COLUMNS = [
    [at(y, z + 4 * k, c) for k in range(Z // 4)]
    for y in range(Y)
    for z in range(4)
    for c in range(C)
]
BASES = [0, 8, 12, 4]
GROUPS = (4, 4, 4, 4)
PARTS = Y * C + len(GROUPS)


def along_z(value, distance, other_distance=None):
    distances = (distance, distance if other_distance is None else other_distance)
    pairs = [
        (at(y, z, c), at((y + distances[c]) % 2, (z + distances[c]) % Z, c))
        for y in range(Y)
        for z in range(Z)
        for c in range(C)
    ]
    return lax.ppermute(value, "ctx", pairs)


def dot(a, b, dims):
    return lax.dot_general(a, b, dims, preferred_element_type=jnp.float32)


def tile_first(place, tile):
    half = TILES // 2
    low = place[4] + 4 * BLOCKS * tile
    high = place[5] + 4 * BLOCKS * (tile - half)
    return jnp.where(tile < half, low, high) * ROWS


def tile_slots(place, tile):
    half = TILES // 2
    residue = jnp.where(tile < half, place[11], 1 - place[11]) - place[12] + Z
    within = lax.rem(tile, half) * (BLOCKS // 2)
    bases = [place[13 + lax.rem(residue + 2 * i, 4)] for i in range(2)]
    return [bases[i % 2] + within + i // 2 for i in range(BLOCKS)]


def slot_rows(slot):
    return pl.ds(pl.multiple_of(slot * ROWS, ROWS), ROWS)


def gather_parts(refs, qd, kv):
    for j in range(Y * C):
        qd[j] = refs[j][...]
    first = 0
    for part in refs[Y * C :]:
        count = part.shape[0]
        for i in range(count):
            kv[(first + i) * ROWS : (first + i + 1) * ROWS, :] = part[i]
        first += count


def doc_start(place, position):
    begin = jnp.zeros_like(position)
    for k in range(6, 9):
        begin = jnp.where(place[k] <= position, jnp.maximum(begin, place[k]), begin)
    return begin


def tile_state(place, j, tile):
    query_first = place[j] * ROWS
    key_first = tile_first(place, tile)
    key_last = key_first + (4 * BLOCKS - 3) * ROWS - 1
    active = (key_first < query_first + ROWS) & (
        key_last >= doc_start(place, query_first)
    )
    return query_first, key_first, active


def tile_mask(place, query_first, key_first):
    row = lax.broadcasted_iota(jnp.int32, (TILE, ROWS), 0)
    key_position = key_first + row + row // ROWS * (3 * ROWS)
    query_position = query_first + lax.broadcasted_iota(jnp.int32, (TILE, ROWS), 1)
    begin = doc_start(place, query_position)
    return (key_position <= query_position) & (key_position >= begin)


def stats_kernel(place, *refs):
    out, qd, kv, top, total, inner = refs[PARTS:]
    gather_parts(refs[:PARTS], qd, kv)

    def query_block(j, _):
        top[...] = jnp.full(top.shape, FLOOR, jnp.float32)
        total[...] = jnp.zeros(total.shape, jnp.float32)
        inner[...] = jnp.zeros(inner.shape, jnp.float32)

        def key_tile(tile, _):
            query_first, key_first, active = tile_state(place, j, tile)

            @pl.when(active)
            def _():
                mask = tile_mask(place, query_first, key_first)
                slots = tile_slots(place, tile)
                spans = [slot_rows(slot) for slot in slots]
                keys = jnp.concatenate([kv[rows, :HD] for rows in spans], axis=0)
                values = jnp.concatenate([kv[rows, HD:] for rows in spans], axis=0)
                for pair in range(GROUP // 2):
                    span = pl.ds(pair * 2 * ROWS, 2 * ROWS)
                    grad_span = pl.ds((GROUP + pair * 2) * ROWS, 2 * ROWS)
                    scores = dot(keys, qd[j, span, :], NT)
                    grad_probs = dot(values, qd[j, grad_span, :], NT)
                    for i in range(2):
                        head = 2 * pair + i
                        lanes = slice(i * ROWS, (i + 1) * ROWS)
                        s = jnp.where(mask, scores[:, lanes], HIDDEN)
                        s = s.reshape(TILE // 8, 8, ROWS)
                        g = grad_probs[:, lanes].reshape(TILE // 8, 8, ROWS)
                        old = top[head]
                        new = jnp.maximum(old, jnp.max(s, axis=0))
                        factor = jnp.exp2((old - new) * POWER)
                        p = jnp.exp2((s - new[None]) * POWER)
                        total[head] = total[head] * factor + jnp.sum(p, axis=0)
                        inner[head] = inner[head] * factor + jnp.sum(p * g, axis=0)
                        top[head] = new

            return 0

        lax.fori_loop(0, TILES, key_tile, 0)
        tops = top[...]
        best = jnp.max(tops, axis=1)
        weight = jnp.exp2((tops - best[:, None, :]) * POWER)
        out[0, j] = best
        out[1, j] = jnp.sum(total[...] * weight, axis=1)
        out[2, j] = jnp.sum(inner[...] * weight, axis=1)
        return 0

    lax.fori_loop(0, Y * C, query_block, 0)


def grads_kernel(place, stats, *refs):
    dq, dq_core = refs[PARTS : PARTS + 2]
    sums, scratch = refs[PARTS + 2 : PARTS + 2 + len(GROUPS)], refs[PARTS + 2 + len(GROUPS) :]
    qd, kv, kt, log_total, delta, probs, grad_scores, dqt, dkv_sum = scratch
    gather_parts(refs[:PARTS], qd, kv)
    for slot in range(Z):
        rows = slice(slot * ROWS, (slot + 1) * ROWS)
        kt[slot] = kv[rows, :HD].T
    mine_y, mine_c = place[9], place[10]
    for j in range(Y * C):
        parts = []
        for r in range(Y * C):
            slot = 2 * (mine_y ^ (r & 1)) + (mine_c ^ (r >> 1))
            parts.append([stats[slot, k, j ^ r] for k in range(3)])
        best = parts[0][0]
        for part in parts[1:]:
            best = jnp.maximum(best, part[0])
        total = jnp.zeros_like(best)
        inner = jnp.zeros_like(best)
        for part in parts:
            weight = jnp.exp2((part[0] - best) * POWER)
            total += part[1] * weight
            inner += part[2] * weight
        log_total[j] = best * POWER + jnp.log(total) * math.log2(math.e)
        delta[j] = inner / total
    dkv_sum[...] = jnp.zeros(dkv_sum.shape, jnp.float32)

    def query_block(j, _):
        dqt[...] = jnp.zeros(dqt.shape, jnp.float32)

        def key_tile(tile, _):
            query_first, key_first, active = tile_state(place, j, tile)

            @pl.when(active)
            def _():
                mask = tile_mask(place, query_first, key_first)
                slots = tile_slots(place, tile)
                spans = [slot_rows(slot) for slot in slots]
                keys = jnp.concatenate([kv[rows, :HD] for rows in spans], axis=0)
                values = jnp.concatenate([kv[rows, HD:] for rows in spans], axis=0)
                for pair in range(GROUP // 2):
                    span = pl.ds(pair * 2 * ROWS, 2 * ROWS)
                    grad_span = pl.ds((GROUP + pair * 2) * ROWS, 2 * ROWS)
                    scores = dot(keys, qd[j, span, :], NT)
                    grads = dot(values, qd[j, grad_span, :], NT)
                    for i in range(2):
                        head = 2 * pair + i
                        lanes = slice(i * ROWS, (i + 1) * ROWS)
                        whole = slice(head * ROWS, (head + 1) * ROWS)
                        x = scores[:, lanes] * POWER - log_total[j, pl.ds(head, 1), :]
                        p = jnp.exp2(jnp.where(mask, x, FLOOR))
                        probs[:, whole] = p.astype(jnp.bfloat16)
                        d = p * (grads[:, lanes] - delta[j, pl.ds(head, 1), :])
                        grad_scores[:, whole] = d.astype(jnp.bfloat16)
                weights = grad_scores[...]
                keys_t = jnp.concatenate([kt[slot] for slot in slots], axis=1)
                dqt[...] += dot(keys_t, weights, NN)
                key_term = dot(weights, qd[j, pl.ds(0, GROUP * ROWS), :], NN)
                value_term = dot(probs[...], qd[j, pl.ds(GROUP * ROWS, GROUP * ROWS), :], NN)
                for i, rows in enumerate(spans):
                    dkv_sum[rows, :HD] += key_term[i * ROWS : (i + 1) * ROWS]
                    dkv_sum[rows, HD:] += value_term[i * ROWS : (i + 1) * ROWS]

            return 0

        lax.fori_loop(0, TILES, key_tile, 0)
        for half, place_of in enumerate((dq, dq_core)):

            @pl.when(j // 2 == half)
            def _():
                for head in range(GROUP):
                    lanes = slice(head * ROWS, (head + 1) * ROWS)
                    turned = dqt[:, lanes].T * SCALE
                    place_of[lax.rem(j, 2), :, lanes] = turned.astype(jnp.bfloat16)

        return 0

    lax.fori_loop(0, Y * C, query_block, 0)
    slot = 0
    for part in sums:
        for i in range(part.shape[0]):
            rows = slice(slot * ROWS, (slot + 1) * ROWS)
            part[i, :, :HD] = (dkv_sum[rows, :HD] * SCALE).astype(jnp.bfloat16)
            part[i, :, HD:] = dkv_sum[rows, HD:].astype(jnp.bfloat16)
            slot += 1


def own_kv_kernel(inputs, weight, keys, out):
    values = dot(inputs[...], weight[...], NN).astype(jnp.bfloat16)
    for k in range(out.shape[0]):
        out[k, :, :HD] = keys[...]
        out[k, :, HD:] = values


def own_queries_kernel(index, labels, segments, queries, grads, out, place):
    context = index[0]
    y, z, c = context // (Z * C), lax.rem(context // C, Z), lax.rem(context, C)
    side = lax.rem(y + z, 2)
    for j in range(Y * C):
        place[j] = at(y ^ (j & 1), z, c ^ (j >> 1))
    place[4] = 2 * side + c
    place[5] = 2 * Z + 2 * (1 - side) + c
    for k in range(1, 4):
        before = jnp.where(segments[...] < k, 1.0, 0.0).astype(jnp.float32)
        place[5 + k] = jnp.sum(before).astype(jnp.int32)
    for i, value in enumerate((y, c, side, z)):
        place[9 + i] = value
    for i, base in enumerate(BASES):
        place[13 + i] = base
    position = context * ROWS + lax.broadcasted_iota(
        jnp.int32, (ROWS, labels.shape[1]), 0
    )
    labelled = jnp.where(position == labels[...], 3.0, 0.0).astype(jnp.float32)
    weight = 1.0 + jnp.max(labelled, axis=1, keepdims=True)
    for head in range(GROUP):
        lanes = slice(head * HD, (head + 1) * HD)
        out[head * ROWS : (head + 1) * ROWS] = queries[:, lanes]
        weighted = grads[:, lanes].astype(jnp.float32) * weight
        out[(GROUP + head) * ROWS : (GROUP + head + 1) * ROWS] = weighted.astype(jnp.bfloat16)


def finish_kernel(place, parts, inputs, weight, key_grad, kept, sent, terms):
    summed = parts[0].astype(jnp.float32)
    for i in range(1, parts.shape[0]):
        summed += parts[i].astype(jnp.float32)
    summed = summed.astype(jnp.bfloat16)
    key_grad[...] = summed[:, :HD]
    value_grad = summed[:, HD:]
    total = dot(value_grad, inputs[...], TN)
    width = kept.shape[1]
    first = place[10] == 0
    for i in range(kept.shape[0]):
        turned = total[:, i * C * width : (i + 1) * C * width].T
        low, high = turned[:width], turned[width:]
        kept[i] = jnp.where(first, low, high).astype(jnp.bfloat16)
        sent[i] = jnp.where(first, high, low).astype(jnp.bfloat16)
    across, lines, _, span = terms.shape
    for x in range(across):
        for h in range(lines):
            rows = slice((h * across + x) * span, (h * across + x + 1) * span)
            terms[x, h] = dot(value_grad, weight[rows, :], NT).astype(jnp.bfloat16)


def on_device(
    sublayer_input,
    rotated_queries,
    rotated_keys,
    output_grad,
    value_weight,
    segment_ids,
    label_positions,
):
    bf16, f32 = jnp.bfloat16, jnp.float32
    context = lax.axis_index("ctx")
    mine_y, mine_c = context // (Z * C), context % C
    smem = pl.BlockSpec(memory_space=pltpu.SMEM)
    vmem = pl.BlockSpec(memory_space=pltpu.VMEM)
    params = pltpu.CompilerParams(vmem_limit_bytes=24 * 1024 * 1024)
    column = pl.pallas_call(
        own_kv_kernel,
        out_shape=jax.ShapeDtypeStruct((Z // 4, ROWS, 2 * HD), bf16),
        in_specs=[vmem] * 3,
        out_specs=vmem,
        compiler_params=params,
    )(sublayer_input, value_weight, rotated_keys)
    column, output_grad, rotated_queries = lax.optimization_barrier(
        (column, output_grad, rotated_queries)
    )
    column = lax.all_to_all(column, "ctx", 0, 0, axis_index_groups=COLUMNS)

    own, place = pl.pallas_call(
        own_queries_kernel,
        out_shape=(
            jax.ShapeDtypeStruct((2 * GROUP * ROWS, HD), bf16),
            jax.ShapeDtypeStruct((13 + len(BASES),), jnp.int32),
        ),
        in_specs=[smem] + [vmem] * 4,
        out_specs=(vmem, smem),
        compiler_params=params,
    )(
        context.astype(jnp.int32).reshape(1),
        label_positions[None],
        segment_ids.reshape(-1, HD),
        rotated_queries,
        output_grad,
    )
    across = lax.ppermute(own, "ctx", Y_SWAP)
    beside = lax.ppermute(own, "ctx", C_SWAP)
    plane = Y * C
    column, beside = lax.optimization_barrier((column, beside))
    kv = [
        column,
        along_z(column, 1),
        along_z(column, -1),
        along_z(column, 2, -2),
    ]
    across, kv = lax.optimization_barrier((across, kv))
    corner = lax.ppermute(across, "ctx", C_SWAP)
    operands = [own, across, beside, corner]
    operands += kv
    stat = pltpu.VMEM((GROUP, 8, ROWS), f32)
    all_qd = pltpu.VMEM((plane, 2 * GROUP * ROWS, HD), bf16)
    all_kv = pltpu.VMEM((Z * ROWS, 2 * HD), bf16)
    stats = pl.pallas_call(
        stats_kernel,
        out_shape=jax.ShapeDtypeStruct((3, plane, GROUP, ROWS), f32),
        in_specs=[smem] + [vmem] * PARTS,
        out_specs=vmem,
        scratch_shapes=[all_qd, all_kv, stat, stat, stat],
        compiler_params=params,
    )(place, *operands)
    all_stats = lax.all_gather(stats, "ctx", axis_index_groups=QUADS)
    dq, dq_core, *sums = pl.pallas_call(
        grads_kernel,
        out_shape=[jax.ShapeDtypeStruct((2, ROWS, GROUP * HD), bf16)] * 2
        + [jax.ShapeDtypeStruct((n, ROWS, 2 * HD), bf16) for n in GROUPS],
        in_specs=[smem, vmem] + [vmem] * PARTS,
        out_specs=[vmem] * (2 + len(GROUPS)),
        scratch_shapes=[
            all_qd,
            all_kv,
            pltpu.VMEM((Z, HD, ROWS), bf16),
            pltpu.VMEM((plane, GROUP, ROWS), f32),
            pltpu.VMEM((plane, GROUP, ROWS), f32),
            pltpu.VMEM((TILE, GROUP * ROWS), bf16),
            pltpu.VMEM((TILE, GROUP * ROWS), bf16),
            pltpu.VMEM((HD, GROUP * ROWS), f32),
            pltpu.VMEM((Z * ROWS, 2 * HD), f32),
        ],
        compiler_params=params,
    )(place, all_stats, *operands)

    back = [along_z(sums[1], -1), along_z(sums[2], 1), along_z(sums[3], -2, 2)]
    column = sums[0].astype(f32)
    for part in back:
        column += part.astype(f32)
    column = lax.all_to_all(column.astype(bf16), "ctx", 0, 0, axis_index_groups=COLUMNS)
    piece = sublayer_input.shape[1] // (Y * Z * C)
    width = value_weight.shape[0] // (2 * X)
    key_grad, kept, sent, terms = pl.pallas_call(
        finish_kernel,
        out_shape=[
            jax.ShapeDtypeStruct((ROWS, HD), bf16),
            jax.ShapeDtypeStruct((Y * Z, piece, HD), bf16),
            jax.ShapeDtypeStruct((Y * Z, piece, HD), bf16),
            jax.ShapeDtypeStruct((X, 2, ROWS, width), bf16),
        ],
        in_specs=[smem] + [vmem] * 3,
        out_specs=[vmem] * 4,
        compiler_params=params,
    )(place, column, sublayer_input, value_weight)
    terms = lax.all_to_all(terms, "mp", 0, 0, axis_index_groups=X_GROUPS)
    terms = jnp.sum(terms.astype(f32), axis=0)
    upper = lax.axis_index("mp") // X == 1
    other = jnp.where(upper, terms[0], terms[1]).astype(bf16)
    other = lax.ppermute(other, "mp", H_SWAP).astype(f32)
    input_grad = (jnp.where(upper, terms[1], terms[0]) + other).astype(bf16)
    near = lax.ppermute(sent, "ctx", C_SWAP)
    term = (kept.astype(f32) + near.astype(f32)).astype(bf16).reshape(Y, Z, piece, HD)
    far = lax.ppermute(jnp.where(mine_y == 0, term[1], term[0]), "ctx", Y_SWAP)
    term = jnp.where(mine_y == 0, term[0], term[1]).astype(f32) + far.astype(f32)
    term = term.astype(bf16)
    from_core = lax.ppermute(dq_core, "ctx", C_SWAP).astype(f32)
    for_across = (dq[1].astype(f32) + from_core[1]).astype(bf16)
    from_across = lax.ppermute(for_across, "ctx", Y_SWAP).astype(f32)
    query_grad = (dq[0].astype(f32) + from_core[0] + from_across).astype(bf16)
    pieces = lax.all_to_all(term, "ctx", 0, 0, axis_index_groups=LINES)
    value_weight_grad = jnp.sum(pieces.astype(f32), axis=0).astype(bf16)
    return (query_grad, key_grad, input_grad, value_weight_grad)


def solution(mesh):
    placed = (
        P("ctx", None),
        P("ctx", "mp"),
        P("ctx", "mp"),
        P("ctx", "mp"),
        P(None, "mp"),
        P(),
        P(),
    )
    return jax.shard_map(
        on_device,
        mesh=mesh,
        in_specs=placed,
        out_specs=(P("ctx", "mp"), P("ctx", "mp"), P("ctx", "mp"), P("ctx", "mp")),
        check_vma=False,
    )
```
